128 devices in a mesh: sim: 32 (over y_hi, z, x), learn: 4 (over y_lo, core).
Axes of the slice: x: 4, y: 4 (y_hi: 2, y_lo: 2; y = y_hi * 2 + y_lo), z: 4, core: 2. Of those that a mesh axis runs over, the one named last changes fastest.
Arguments:
- fields: float32 [8, 256, 32, 128], P(None, 'sim', 'learn'), may hold values from -2.2 to 2.2
- diffusivity: float32 [8], replicated, may hold values from 0.5 to 1.6
- stoich: float32 [8], replicated, may hold values from -1 to 1
- basis: bfloat16 [96, 8, 256, 32, 128], P(None, None, 'sim', 'learn'), may hold values from -0.006214806 to 0.006214806
- gram_old: float32 [96, 96], replicated, may hold values from -6 to 6
Outputs:
- final_fields: float32 [8, 256, 32, 128], P(None, 'sim', 'learn')
- reduced: float32 [96, 8], replicated
- pod_gram: float32 [96, 96], replicated
- rhs_block: float32 [4752, 96], P('learn')
The draws below stay inside these ranges and needn't reach their ends.
All inputs are finite; a program needn't handle non-finite values.
Results may differ from the reference program's by a relative error of at most 0.0077.
Values sent between devices are 32-bit elements; how exact they have to be, the bound alone decides.
A program may use at most 64 MiB of HBM per device.

```python
import math
import jax
import jax.numpy as jnp
import numpy as np
from jax import lax

NF = 8
MODES = 96
STEPS = 8
CX = 8
CY = 8
NX = 256
NY = 32
NZ = 128


def draw_fields(key, part):
    shape = (NF, NX, NY, NZ)
    along_x = jnp.arange(NX, dtype=jnp.int32)
    along_y = jnp.arange(NY, dtype=jnp.int32)
    along_z = jnp.arange(NZ, dtype=jnp.int32)
    parity = (along_x[:, None, None] + along_y[None, :, None] + along_z[None, None, :]) % 2
    alternate = 1.0 - 2.0 * parity.astype(jnp.float32)
    magnitude = jax.random.uniform(key, shape, jnp.float32, 0.6, 2.2)
    values = alternate[None] * magnitude
    return values


def draw_diffusivity(key, part):
    uniform_draw = jax.random.uniform(key, (NF,), jnp.float32, 0.0, 1.1)
    spread = jnp.max(uniform_draw) - uniform_draw
    result_values = 1.6 * jnp.exp(-spread)
    return result_values


def draw_basis(key, part):
    shape = (MODES, NF, NX, NY, NZ)
    entries = jnp.clip(jax.random.normal(key, shape, jnp.float32), -6.0, 6.0)
    along_x = jnp.arange(NX, dtype=jnp.int32) % CX
    along_y = jnp.arange(NY, dtype=jnp.int32) % CY
    edge_x = (along_x == 0) | (along_x == CX - 1)
    edge_y = (along_y == 0) | (along_y == CY - 1)
    on_face = edge_x[:, None] | edge_y[None, :]
    factor = jnp.where(on_face, 3.0, 1.0).astype(jnp.float32)
    face_count = CX * CY - max(CX - 2, 0) * max(CY - 2, 0)
    total_weight = NX // CX * (NY // CY) * (9 * face_count + CX * CY - face_count) * NF * NZ
    return (entries * factor[None, None, :, :, None] / math.sqrt(total_weight)).astype(jnp.bfloat16)


def scatter_about(stream_key, shape, scale, limit, kind=jnp.bfloat16):
    drawn = jax.random.normal(stream_key, shape, jnp.float32) * scale
    return jnp.minimum(jnp.maximum(drawn, -limit), limit).astype(kind)


def setup_inputs(seed: int = 0) -> dict:
    seeds = jax.random.split(jax.random.key(seed), 6)
    return {
        "fields": draw_fields(jax.random.fold_in(seeds[5], 71), 0),
        "diffusivity": draw_diffusivity(jax.random.fold_in(seeds[5], 71), 0),
        "stoich": jnp.clip(jax.random.uniform(seeds[2], (NF,), jnp.float32, -1.0, 1.0), -1.0, 1.0),
        "basis": draw_basis(jax.random.fold_in(seeds[5], 71), 0),
        "gram_old": scatter_about(seeds[4], (MODES, MODES), 1.0, 6.0, jnp.float32),
    }


time_step = 0.1
drift_x = 1.2
drift_y = 1.0
drift_z = 0.3
arrhenius = 2.0
activation = 1.0


def tendency(padded, diffusivity, stoich):
    centre = padded[:, 1:-1, 1:-1, 1:-1]
    east = padded[:, 2:, 1:-1, 1:-1]
    west = padded[:, :-2, 1:-1, 1:-1]
    north = padded[:, 1:-1, 2:, 1:-1]
    south = padded[:, 1:-1, :-2, 1:-1]
    upper = padded[:, 1:-1, 1:-1, 2:]
    lower = padded[:, 1:-1, 1:-1, :-2]
    laplace = east + west + north + south + upper + lower - 6.0 * centre
    advect = drift_x * 0.5 * (east - west) + drift_y * 0.5 * (north - south) + drift_z * 0.5 * (upper - lower)
    reaction = arrhenius * jnp.tanh(centre[0]) * jnp.tanh(centre[1]) * jnp.exp(-activation / (1.0 + centre[7] * centre[7]))
    return diffusivity[:, None, None, None] * laplace - advect + stoich[:, None, None, None] * reaction[None]


def pad_cells(state):
    return jnp.pad(state, ((0, 0), (1, 1), (1, 1), (1, 1)))


def pair_tables(modes):
    upper_pairs = np.triu_indices(modes)
    first_table = np.concatenate([np.zeros(modes), upper_pairs[0] + 1]).astype(np.int32)
    second_table = np.concatenate([np.arange(modes) + 1, upper_pairs[1] + 1]).astype(np.int32)
    return first_table, second_table


def reference(fields, diffusivity, stoich, basis, gram_old):
    state = fields
    snapshots = []
    for counter in range(STEPS):
        first = tendency(pad_cells(state), diffusivity, stoich)
        middle = state + time_step * first
        second = tendency(pad_cells(middle), diffusivity, stoich)
        state = state + 0.5 * time_step * (first + second)
        snapshots.append(state.astype(jnp.bfloat16).reshape(1, -1))
    stacked = jnp.concatenate(snapshots, axis=0)
    flat_basis = basis.reshape(MODES, -1)
    reduced = lax.dot_general(flat_basis, stacked, (((1,), (1,)), ((), ())), preferred_element_type=jnp.float32)
    pod_gram = gram_old + jnp.dot(reduced, reduced.T, precision=lax.Precision.HIGHEST, preferred_element_type=jnp.float32)
    widened = jnp.concatenate([jnp.ones((1, STEPS), jnp.float32), reduced], axis=0)
    first_table, second_table = pair_tables(MODES)
    features = widened[first_table, :-1] * widened[second_table, :-1]
    changes = reduced[:, 1:] - reduced[:, :-1]
    rhs_block = jnp.dot(features, changes.T, precision=lax.Precision.HIGHEST, preferred_element_type=jnp.float32)
    return state, reduced, pod_gram, rhs_block
```

```python
import functools

import jax
import jax.numpy as jnp
import numpy as np
from jax import lax
from jax.experimental import pallas as pl
from jax.experimental.pallas import tpu as pltpu
from jax.sharding import PartitionSpec as P

MESH = pl.DeviceIdType.MESH
STEPS = 8
PER = 1
W = 2 * PER
NF = 8
CX = 8
CY = 8
XB = CX + 2 * W
YB = CY + 2 * W
MODES = 96
F32 = jnp.float32
BF16 = jnp.bfloat16

time_step = 0.1
drift_x = 1.2
drift_y = 1.0
drift_z = 0.3
arrhenius = 2.0
activation = 1.0

DIRS = [(dx, dy) for dx in (-1, 0, 1) for dy in (-1, 0, 1) if (dx, dy) != (0, 0)]


def face_range(d):
    if d < 0:
        return W, W + CX, W
    if d > 0:
        return CX, 0, W
    return W, W, CX


def pieces():
    out = []
    for dx, dy in DIRS:
        if dx == 0 or dy == 0:
            sx, tx, nx = face_range(dx)
            sy, ty, ny = face_range(dy)
            out.append((dx, dy, sx, sy, tx, ty, nx, ny))
            continue
        for i in range(1, W):
            n = W - i
            sx, tx = (W + i - 1, W + CX + i - 1) if dx < 0 else (W + CX - i, W - i)
            sy, ty = (W, W + CY) if dy < 0 else (W + CY - n, W - n)
            out.append((dx, dy, sx, sy, tx, ty, 1, n))
    return out


PIECES = pieces()


def steps_kernel(
    dims,
    diff_ref,
    stoich_ref,
    fields_ref,
    basis_ref,
    final_ref,
    red_ref,
    state,
    mid,
    rate,
    snaps,
    basis,
    acc,
    part,
    slots_a,
    slots_b,
    basis_sem,
    send_sem,
    recv_sem,
    send_a,
    recv_a,
    send_b,
    recv_b,
):
    (yh_n, z_n, x_n), (yl_n, core_n) = dims
    sims, learns = yh_n * z_n * x_n, yl_n * core_n
    s = lax.axis_index("sim")
    l = lax.axis_index("learn")

    fetch = pltpu.make_async_copy(basis_ref, basis, basis_sem)
    fetch.start()

    state[...] = jnp.zeros_like(state)
    mid[...] = jnp.zeros_like(mid)

    x_me = s % x_n
    z_me = (s // x_n) % z_n
    yh_me = s // (x_n * z_n)
    core_me = l % core_n
    yl_me = l // core_n

    peers_a = []
    na = x_n * core_n
    rank_a = x_me * core_n + core_me
    for k in range(1, na):
        r = (rank_a + k) % na
        peers_a.append(((s - x_me) + r // core_n, (l - core_me) + r % core_n))
    peers_b = []
    nb = yh_n * z_n * yl_n
    rank_b = (yh_me * z_n + z_me) * yl_n + yl_me
    for k in range(1, nb):
        r = (rank_b + k) % nb
        yz = r // yl_n
        peers_b.append((yz * x_n + x_me, (r % yl_n) * core_n + core_me))

    def there(dx, dy):
        ok = None
        for d, me, n in ((dx, s, sims), (dy, l, learns)):
            if d == 0:
                continue
            c = me > 0 if d < 0 else me < n - 1
            ok = c if ok is None else ok & c
        return ok

    barrier = pltpu.get_barrier_semaphore()
    count = jnp.int32(len(peers_a) + len(peers_b))
    for dx, dy in DIRS:
        ok = there(dx, dy)
        count = count + ok.astype(jnp.int32)

        @pl.when(ok)
        def _(dx=dx, dy=dy):
            pl.semaphore_signal(
                barrier, inc=1, device_id={"sim": s + dx, "learn": l + dy}, device_id_type=MESH
            )

    for ps, pl_ in peers_a + peers_b:
        pl.semaphore_signal(barrier, inc=1, device_id={"sim": ps, "learn": pl_}, device_id_type=MESH)

    for f in range(NF):
        for x in range(CX):
            state[W + x, pl.ds(W * 8 + f, 8, stride=8), :] = fields_ref[f * CX + x]

    row = lax.broadcasted_iota(jnp.int32, (8, 128), 0)
    lane = lax.broadcasted_iota(jnp.int32, (8, 128), 1)
    diff = jnp.zeros((8, 128), F32)
    sto = jnp.zeros((8, 128), F32)
    for f in range(NF):
        diff = jnp.where(row == f, diff_ref[f], diff)
        sto = jnp.where(row == f, stoich_ref[f], sto)

    def coefs(scale, keep):
        upper = jnp.where(lane < 127, scale * (diff - 0.5 * drift_z), 0.0)
        lower = jnp.where(lane > 0, scale * (diff + 0.5 * drift_z), 0.0)
        return (
            keep - (6.0 * scale) * diff,
            scale * (diff - 0.5 * drift_x),
            scale * (diff + 0.5 * drift_x),
            scale * (diff - 0.5 * drift_y),
            scale * (diff + 0.5 * drift_y),
            upper,
            lower,
            (scale * arrhenius) * sto,
        )

    coefs_1 = coefs(time_step, 1.0)
    coefs_2 = coefs(0.5 * time_step, 0.5)

    y_low = jnp.where(l > 0, 1.0, 0.0).astype(F32)
    y_high = jnp.where(l < learns - 1, 1.0, 0.0).astype(F32)

    def rates(src, base, r):
        starts = sorted({W - r + 8 * i for i in range((CY + 2 * r) // 8)} | {W + r})
        for x in range(W - r, W + CX + r):
            for y in starts:
                u0 = src[base + x, pl.ds(y * 8, 8, stride=8), :]
                u1 = src[base + x, pl.ds(y * 8 + 1, 8, stride=8), :]
                u7 = src[base + x, pl.ds(y * 8 + 7, 8, stride=8), :]
                rate[x, pl.ds(y, 8), :] = (
                    jnp.tanh(u0) * jnp.tanh(u1) * jnp.exp(-activation / (1.0 + u7 * u7))
                )

    def stage(src, base, dst, dbase, r, cs, old=None, obase=0):
        c_c, c_e, c_w, c_n, c_s, c_u, c_l, c_r = cs
        rates(src, base, r)
        lo = jnp.where(s > 0, W - r, W)
        hi = jnp.where(s < sims - 1, W + CX + r, W + CX)

        def line(x, _):
            cells = {y: src[base + x, pl.ds(y * 8, 8), :] for y in range(W - r - 1, W + CY + r + 1)}
            for y in range(W - r, W + CY + r):
                c = cells[y]
                east = src[base + x + 1, pl.ds(y * 8, 8), :]
                west = src[base + x - 1, pl.ds(y * 8, 8), :]
                q = jnp.broadcast_to(rate[x, pl.ds(y, 1), :], (8, 128))
                v = (c_c * c + c_e * east) + (c_w * west + c_n * cells[y + 1])
                v2 = (c_s * cells[y - 1] + c_r * q) + (
                    c_u * pltpu.roll(c, 127, 1) + c_l * pltpu.roll(c, 1, 1)
                )
                v = v + v2
                if old is not None:
                    v = v + 0.5 * old[obase + x, pl.ds(y * 8, 8), :]
                if y < W:
                    v = v * y_low
                if y >= W + CY:
                    v = v * y_high
                dst[dbase + x, pl.ds(y * 8, 8), :] = v
            return 0

        lax.fori_loop(lo, hi, line, 0)

    def snapshot(base, t):
        for fp in range(NF // 2):
            for xp in range(CX // 2):
                halves = []
                for f in (2 * fp, 2 * fp + 1):
                    a = state[base + W + 2 * xp, pl.ds(W * 8 + f, 8, stride=8), :]
                    b = state[base + W + 2 * xp + 1, pl.ds(W * 8 + f, 8, stride=8), :]
                    halves.append(jnp.concatenate([a, b], axis=0))
                tile = jnp.concatenate(halves, axis=1).astype(BF16)
                snaps[fp * 4 + xp, pl.ds(pl.multiple_of(t * 16, 16), 16), :] = tile

    def copy(par, k):
        dx, dy, sx, sy, tx, ty, nx, ny = PIECES[k]
        return pltpu.make_async_remote_copy(
            src_ref=state.at[pl.ds(par * XB + sx, nx), pl.ds(sy * 8, ny * 8), :],
            dst_ref=state.at[pl.ds(par * XB + tx, nx), pl.ds(ty * 8, ny * 8), :],
            send_sem=send_sem.at[par, k],
            recv_sem=recv_sem.at[par, k],
            device_id={"sim": s + dx, "learn": l + dy},
            device_id_type=MESH,
        )

    pl.semaphore_wait(barrier, count)

    def window(e, _):
        par = lax.rem(e, 2)
        base = par * XB
        nxt = (1 - par) * XB
        for k, p in enumerate(PIECES):

            @pl.when(there(p[0], p[1]))
            def _(k=k):
                copy(par, k).start()

        for k, p in enumerate(PIECES):

            @pl.when(there(-p[0], -p[1]))
            def _(k=k):
                copy(par, k).wait_recv()

        stage(state, base, mid, 0, 1, coefs_1)
        stage(mid, 0, state, nxt, 0, coefs_2, state, base)
        snapshot(nxt, e)
        for k, p in enumerate(PIECES):

            @pl.when(there(p[0], p[1]))
            def _(k=k):
                copy(par, k).wait_send()

        return 0

    lax.fori_loop(0, STEPS, window, 0)

    fetch.wait()
    acc[...] = jnp.zeros_like(acc)

    def block(kb, _):
        fp = kb // 4
        xp = kb % 4
        r0 = pl.multiple_of(fp * 128 + xp * 16, 16)
        lhs = jnp.concatenate(
            [
                basis[:, pl.ds(r0, 16), :].reshape(MODES * 16, 128),
                basis[:, pl.ds(r0 + 64, 16), :].reshape(MODES * 16, 128),
            ],
            axis=1,
        )
        acc[...] += lax.dot_general(
            lhs, snaps[kb], (((1,), (1,)), ((), ())), preferred_element_type=F32
        )
        return 0

    lax.fori_loop(0, 16, block, 0)

    last = (STEPS % 2) * XB
    for f in range(NF):
        for x in range(CX):
            final_ref[f * CX + x] = state[last + W + x, pl.ds(W * 8 + f, 8, stride=8), :]

    r16 = lax.broadcasted_iota(jnp.int32, (16, 128), 0)
    c16 = lax.broadcasted_iota(jnp.int32, (16, 128), 1)
    diagonal = (c16 % 16 == r16).astype(F32)
    kept = jnp.sum(acc[...].reshape(MODES, 16, 128) * diagonal[None], axis=1)
    kept = jnp.concatenate([kept, jnp.zeros((128 - MODES, 128), F32)], axis=0)
    groups = (lane // 16 == row).astype(F32)
    mine = lax.dot_general(
        groups,
        kept,
        (((1,), (1,)), ((), ())),
        precision=lax.Precision.HIGHEST,
        preferred_element_type=F32,
    )

    def share(slots, peers, rank, n, phase, send, recv):
        copies = []
        for k, (ps, pl_) in enumerate(peers):
            c = pltpu.make_async_remote_copy(
                src_ref=part.at[phase],
                dst_ref=slots.at[k],
                send_sem=send.at[k],
                recv_sem=recv.at[k],
                device_id={"sim": ps, "learn": pl_},
                device_id_type=MESH,
            )
            c.start()
            copies.append(c)
        for c in copies:
            c.wait()

    def total(slots, rank, n, phase):
        out = jnp.zeros((8, 128), F32)
        for r in range(n):
            k = lax.rem(rank - r + n - 1 + n, n)
            mine_now = part[phase]
            other = slots[jnp.minimum(k, n - 2)]
            out = out + jnp.where(rank == r, mine_now, other)
        return out

    part[0] = mine
    share(slots_a, peers_a, rank_a, na, 0, send_a, recv_a)
    part[1] = total(slots_a, rank_a, na, 0)
    share(slots_b, peers_b, rank_b, nb, 1, send_b, recv_b)
    red_ref[...] = total(slots_b, rank_b, nb, 1)


def split3(v):
    hi = v.astype(BF16).astype(F32)
    rest = v - hi
    mi = rest.astype(BF16).astype(F32)
    return hi, mi, rest - mi


def outer_sum(a, b):
    ah, am, al = split3(a)
    bh, bm, bl = split3(b)
    left = jnp.concatenate([ah, ah, am, am, ah, al], axis=0).astype(BF16)
    right = jnp.concatenate([bh, bm, bh, bm, bl, bh], axis=0).astype(BF16)
    return lax.dot_general(left, right, (((0,), (0,)), ((), ())), preferred_element_type=F32)


def tail_kernel(rows, red_ref, gram_ref, first_ref, second_ref, reduced_ref, pod_ref, rhs_ref):
    l = lax.axis_index("learn")
    red = red_ref[...]
    row = lax.broadcasted_iota(jnp.int32, (8, 128), 0)
    lane = lax.broadcasted_iota(jnp.int32, (8, 128), 1)
    reduced_ref[...] = red.T[:MODES]
    pod_ref[...] = gram_ref[...] + outer_sum(red, red)[:MODES, :MODES]
    widened = jnp.where(lane == 0, 1.0, pltpu.roll(red, 1, 1))
    changes = jnp.where(row < STEPS - 1, pltpu.roll(red, 7, 0) - red, 0.0)
    feats = []
    for j in range(first_ref.shape[1]):
        one = jnp.broadcast_to(first_ref[l, pl.ds(j, 1), :], (8, 128))
        two = jnp.broadcast_to(second_ref[l, pl.ds(j, 1), :], (8, 128))
        feats.append(
            jnp.take_along_axis(widened, one, axis=1, mode="promise_in_bounds")
            * jnp.take_along_axis(widened, two, axis=1, mode="promise_in_bounds")
        )
    feats = jnp.concatenate(feats, axis=1)
    rhs_ref[...] = outer_sum(feats, changes)[:rows, :MODES]


def pair_tables(modes, blocks):
    upper_pairs = np.triu_indices(modes)
    first = np.concatenate([np.zeros(modes), upper_pairs[0] + 1]).astype(np.int32)
    second = np.concatenate([np.arange(modes) + 1, upper_pairs[1] + 1]).astype(np.int32)
    rows = first.shape[0] // blocks
    lines = -(-rows // 128)

    def lay(t):
        t = t.reshape(blocks, rows)
        t = np.pad(t, ((0, 0), (0, lines * 128 - rows)))
        return t.reshape(blocks, lines, 128)

    return rows, lay(first), lay(second)


def solution(mesh):
    sims, learns = mesh.shape["sim"], mesh.shape["learn"]
    dims = ((2, 4, 4), (2, 2)) if (sims, learns) == (32, 4) else ((1, 1, sims), (1, learns))
    (yh_n, z_n, x_n), (yl_n, core_n) = dims
    na, nb = x_n * core_n, yh_n * z_n * yl_n
    rows, first, second = pair_tables(MODES, learns)
    vmem = pl.BlockSpec(memory_space=pltpu.VMEM)
    smem = pl.BlockSpec(memory_space=pltpu.SMEM)
    n_pieces = len(PIECES)

    def body(fields, diffusivity, stoich, basis, gram_old):
        flat = basis.reshape(MODES, NF * CX * CY, 128)
        final, red = pl.pallas_call(
            functools.partial(steps_kernel, dims),
            out_shape=(
                jax.ShapeDtypeStruct((NF * CX, CY, 128), F32),
                jax.ShapeDtypeStruct((8, 128), F32),
            ),
            in_specs=[smem, smem, vmem, pl.BlockSpec(memory_space=pl.ANY)],
            out_specs=(vmem, vmem),
            scratch_shapes=[
                pltpu.VMEM((2 * XB, YB * 8, 128), F32),
                pltpu.VMEM((XB, YB * 8, 128), F32),
                pltpu.VMEM((XB, -(-YB // 8) * 8, 128), F32),
                pltpu.VMEM((16, 128, 256), BF16),
                pltpu.VMEM((MODES, NF * CX * CY, 128), BF16),
                pltpu.VMEM((MODES * 16, 128), F32),
                pltpu.VMEM((2, 8, 128), F32),
                pltpu.VMEM((max(na - 1, 1), 8, 128), F32),
                pltpu.VMEM((max(nb - 1, 1), 8, 128), F32),
                pltpu.SemaphoreType.DMA,
                pltpu.SemaphoreType.DMA((2, n_pieces)),
                pltpu.SemaphoreType.DMA((2, n_pieces)),
                pltpu.SemaphoreType.DMA((max(na - 1, 1),)),
                pltpu.SemaphoreType.DMA((max(na - 1, 1),)),
                pltpu.SemaphoreType.DMA((max(nb - 1, 1),)),
                pltpu.SemaphoreType.DMA((max(nb - 1, 1),)),
            ],
            compiler_params=pltpu.CompilerParams(
                collective_id=0, has_side_effects=True, vmem_limit_bytes=44 * 1024 * 1024
            ),
            name="steps",
        )(diffusivity, stoich, fields.reshape(NF * CX, CY, 128), flat)
        reduced, pod, rhs = pl.pallas_call(
            functools.partial(tail_kernel, rows),
            out_shape=(
                jax.ShapeDtypeStruct((MODES, STEPS), F32),
                jax.ShapeDtypeStruct((MODES, MODES), F32),
                jax.ShapeDtypeStruct((rows, MODES), F32),
            ),
            in_specs=[vmem] * 4,
            out_specs=(vmem,) * 3,
            name="tail",
        )(red, gram_old, jnp.asarray(first), jnp.asarray(second))
        return final.reshape(NF, CX, CY, 128), reduced, pod, rhs

    in_specs = (
        P(None, "sim", "learn", None),
        P(),
        P(),
        P(None, None, "sim", "learn", None),
        P(),
    )
    out_specs = (P(None, "sim", "learn", None), P(), P(), P("learn", None))
    return jax.shard_map(body, mesh=mesh, in_specs=in_specs, out_specs=out_specs, check_vma=False)
```

```python
import functools

import jax
import jax.numpy as jnp
import numpy as np
from jax import lax
from jax.experimental import pallas as pl
from jax.experimental.pallas import tpu as pltpu
from jax.sharding import PartitionSpec as P

MESH = pl.DeviceIdType.MESH
STEPS = 8
PER = 4
W = 2 * PER
NF = 8
CX = 8
CY = 8
XB = CX + 2 * W
YB = CY + 2 * W
MODES = 96
F32 = jnp.float32
BF16 = jnp.bfloat16

time_step = 0.1
drift_x = 1.2
drift_y = 1.0
drift_z = 0.3
arrhenius = 2.0
activation = 1.0

SIDES = ((-1, 0), (1, 0), (0, -1), (0, 1))

CORNERS = {2: ((1, 1, 1),), 4: ((1, 3, 3),), 6: ((1, 5, 5),), 8: ((1, 4, 7), (5, 7, 3))}[W]


def face_range(d):
    if d < 0:
        return W, W + CX, W
    if d > 0:
        return CX, 0, W
    return W, W, CX


def pieces():
    out = []
    for dx, dy in SIDES:
        sx, tx, nx = face_range(dx)
        sy, ty, ny = face_range(dy)
        out.append((dx, dy, 0, sx, sy, tx, ty, nx, ny))
    for side in (-1, 1):
        for dy in (-1, 1):
            for i0, i1, n in CORNERS:
                x = W - i1 if side < 0 else W + CX + i0 - 1
                sy, ty = (W, W + CY) if dy < 0 else (W + CY - n, W - n)
                out.append((0, dy, side, x, sy, x, ty, i1 - i0 + 1, n))
    return out


PIECES = pieces()


def steps_kernel(
    dims,
    diff_hbm,
    stoich_hbm,
    fields_hbm,
    basis_ref,
    final_ref,
    red_ref,
    state,
    mid,
    later,
    rate,
    snaps,
    basis,
    acc,
    diff_ref,
    stoich_ref,
    fields_ref,
    in_sem,
    part,
    slots_a,
    slots_b,
    basis_sem,
    send_sem,
    recv_sem,
    send_a,
    recv_a,
    send_b,
    recv_b,
):
    (yh_n, z_n, x_n), (yl_n, core_n) = dims
    sims, learns = yh_n * z_n * x_n, yl_n * core_n
    s = lax.axis_index("sim")
    l = lax.axis_index("learn")

    fetch = pltpu.make_async_copy(basis_ref, basis, basis_sem)
    loads = [
        pltpu.make_async_copy(a, b, in_sem.at[i])
        for i, (a, b) in enumerate(
            ((fields_hbm, fields_ref), (diff_hbm, diff_ref), (stoich_hbm, stoich_ref))
        )
    ]
    for c in loads:
        c.start()
    fetch.start()

    for par in range(2):
        for edge, x in ((s == 0, par * XB), (s == lax.axis_size("sim") - 1, par * XB + W + CX)):

            @pl.when(edge)
            def _(x=x):
                state[pl.ds(x, W)] = jnp.zeros((W, YB * 8, 128), F32)

        for edge, y in ((l == 0, 0), (l == lax.axis_size("learn") - 1, W + CY)):

            @pl.when(edge)
            def _(par=par, y=y):
                state[pl.ds(par * XB, XB), pl.ds(y * 8, W * 8), :] = jnp.zeros((XB, W * 8, 128), F32)

    x_me = s % x_n
    z_me = (s // x_n) % z_n
    yh_me = s // (x_n * z_n)
    core_me = l % core_n
    yl_me = l // core_n

    peers_a = []
    na = x_n * core_n
    rank_a = x_me * core_n + core_me
    for k in range(1, na):
        r = (rank_a + k) % na
        peers_a.append(((s - x_me) + r // core_n, (l - core_me) + r % core_n))
    peers_b = []
    nb = yh_n * z_n * yl_n
    rank_b = (yh_me * z_n + z_me) * yl_n + yl_me
    for k in range(1, nb):
        r = (rank_b + k) % nb
        yz = r // yl_n
        peers_b.append((yz * x_n + x_me, (r % yl_n) * core_n + core_me))

    def there(dx, dy):
        ok = None
        for d, me, n in ((dx, s, sims), (dy, l, learns)):
            if d == 0:
                continue
            c = me > 0 if d < 0 else me < n - 1
            ok = c if ok is None else ok & c
        return ok

    barrier = pltpu.get_barrier_semaphore()
    count = jnp.int32(len(peers_a) + len(peers_b))
    for dx, dy in SIDES:
        ok = there(dx, dy)
        count = count + ok.astype(jnp.int32)

        @pl.when(ok)
        def _(dx=dx, dy=dy):
            pl.semaphore_signal(
                barrier, inc=1, device_id={"sim": s + dx, "learn": l + dy}, device_id_type=MESH
            )

    for ps, pl_ in peers_a + peers_b:
        pl.semaphore_signal(barrier, inc=1, device_id={"sim": ps, "learn": pl_}, device_id_type=MESH)

    for c in loads:
        c.wait()

    for f in range(NF):
        for x in range(CX):
            state[W + x, pl.ds(W * 8 + f, 8, stride=8), :] = fields_ref[f * CX + x]

    row = lax.broadcasted_iota(jnp.int32, (8, 128), 0)
    lane = lax.broadcasted_iota(jnp.int32, (8, 128), 1)
    diff = jnp.zeros((8, 128), F32)
    sto = jnp.zeros((8, 128), F32)
    for f in range(NF):
        diff = jnp.where(row == f, diff_ref[f], diff)
        sto = jnp.where(row == f, stoich_ref[f], sto)

    def coefs(scale, keep):
        upper = jnp.where(lane < 127, scale * (diff - 0.5 * drift_z), 0.0)
        lower = jnp.where(lane > 0, scale * (diff + 0.5 * drift_z), 0.0)
        return (
            keep - (6.0 * scale) * diff,
            scale * (diff - 0.5 * drift_x),
            scale * (diff + 0.5 * drift_x),
            scale * (diff - 0.5 * drift_y),
            scale * (diff + 0.5 * drift_y),
            upper,
            lower,
            (scale * arrhenius) * sto,
        )

    coefs_1 = coefs(time_step, 1.0)
    coefs_2 = coefs(0.5 * time_step, 0.5)

    x_low = jnp.where(s > 0, 1.0, 0.0).astype(F32)
    x_high = jnp.where(s < sims - 1, 1.0, 0.0).astype(F32)
    y_low = jnp.where(l > 0, 1.0, 0.0).astype(F32)
    y_high = jnp.where(l < learns - 1, 1.0, 0.0).astype(F32)

    def lines(r):
        for x in range(W - r, W + CX + r):
            beyond = max(W - x, x - (W + CX - 1), 0)
            yield x, W - (r - beyond), W + CY + (r - beyond)

    def rates(src, base, r):
        for x, y0, y1 in lines(r):
            for y in sorted({min(y, y1 - 8) for y in range(y0, y1, 8)}):
                u0 = src[base + x, pl.ds(y * 8, 8, stride=8), :]
                u1 = src[base + x, pl.ds(y * 8 + 1, 8, stride=8), :]
                u7 = src[base + x, pl.ds(y * 8 + 7, 8, stride=8), :]
                rate[x, pl.ds(y, 8), :] = (
                    jnp.tanh(u0) * jnp.tanh(u1) * jnp.exp(-activation / (1.0 + u7 * u7))
                )

    def stage(src, base, dst, dbase, r, cs, old=None, obase=0):
        c_c, c_e, c_w, c_n, c_s, c_u, c_l, c_r = (c[None] for c in cs)
        rates(src, base, r)

        def cells(ref, x, y, n):
            return ref[x, pl.ds(y * 8, n * 8), :].reshape(n, 8, 128)

        for x, y0, y1 in lines(r):
            cuts = sorted({y0, y1} | {y for y in (W, W + CY) if y0 < y < y1})
            for y, end in zip(cuts[:-1], cuts[1:]):
                n = end - y
                c = cells(src, base + x, y, n)
                q = jnp.stack(
                    [jnp.broadcast_to(rate[x, pl.ds(y + j, 1), :], (8, 128)) for j in range(n)]
                )
                v = c_c * c + c_e * cells(src, base + x + 1, y, n)
                v = v + (c_w * cells(src, base + x - 1, y, n) + c_n * cells(src, base + x, y + 1, n))
                v = v + (c_s * cells(src, base + x, y - 1, n) + c_r * q)
                v = v + (c_u * pltpu.roll(c, 127, 2) + c_l * pltpu.roll(c, 1, 2))
                if old is not None:
                    v = v + 0.5 * cells(old, obase + x, y, n)
                masks = []
                if x < W:
                    masks.append(x_low)
                if x >= W + CX:
                    masks.append(x_high)
                if y < W:
                    masks.append(y_low)
                if y >= W + CY:
                    masks.append(y_high)
                if masks:
                    v = v * functools.reduce(lambda a, b: a * b, masks)
                dst[dbase + x, pl.ds(y * 8, n * 8), :] = v.reshape(n * 8, 128)

    def snapshot(src, base, t):
        for fp in range(NF // 2):
            for xp in range(CX // 2):
                halves = []
                for f in (2 * fp, 2 * fp + 1):
                    a = src[base + W + 2 * xp, pl.ds(W * 8 + f, 8, stride=8), :]
                    b = src[base + W + 2 * xp + 1, pl.ds(W * 8 + f, 8, stride=8), :]
                    halves.append(jnp.concatenate([a, b], axis=0))
                tile = jnp.concatenate(halves, axis=1).astype(BF16)
                snaps[fp * 4 + xp, pl.ds(pl.multiple_of(t * 16, 16), 16), :] = tile

    def copy(par, k):
        dx, dy, _, sx, sy, tx, ty, nx, ny = PIECES[k]
        return pltpu.make_async_remote_copy(
            src_ref=state.at[pl.ds(par * XB + sx, nx), pl.ds(sy * 8, ny * 8), :],
            dst_ref=state.at[pl.ds(par * XB + tx, nx), pl.ds(ty * 8, ny * 8), :],
            send_sem=send_sem.at[par, k],
            recv_sem=recv_sem.at[par, k],
            device_id={"sim": s + dx, "learn": l + dy},
            device_id_type=MESH,
        )

    pl.semaphore_wait(barrier, count)

    def window(e, _):
        par = lax.rem(e, 2)
        base = par * XB
        nxt = (1 - par) * XB

        def each(chosen, act, arriving):
            for k in chosen:
                dx, dy, side = PIECES[k][:3]
                ok = there(-dx, -dy) if arriving else there(dx, dy)
                if side:
                    ok = ok & there(side, 0)

                @pl.when(ok)
                def _(k=k):
                    act(copy(par, k))

        every = range(len(PIECES))
        send = lambda c: c.start()
        arrive = lambda c: c.wait_recv()
        each(range(4), send, False)
        for face, side in ((1, -1), (0, 1)):
            each([face], arrive, True)
            each([k for k in every if PIECES[k][2] == side], send, False)
        each(range(2, len(PIECES)), arrive, True)

        src, sbase = state, base
        for k in range(PER):
            r = W - 2 * k
            stage(src, sbase, mid, 0, r - 1, coefs_1)
            dst, dbase = (state, nxt) if k == PER - 1 else (later, (k % 2) * XB)
            stage(mid, 0, dst, dbase, r - 2, coefs_2, src, sbase)
            snapshot(dst, dbase, e * PER + k)
            src, sbase = dst, dbase
        each(every, lambda c: c.wait_send(), False)
        return 0

    lax.fori_loop(0, STEPS // PER, window, 0)

    fetch.wait()
    acc[...] = jnp.zeros_like(acc)

    def block(kb, _):
        fp = kb // 4
        xp = kb % 4
        r0 = pl.multiple_of(fp * 128 + xp * 16, 16)
        lhs = jnp.concatenate(
            [
                basis[:, pl.ds(r0, 16), :].reshape(MODES * 16, 128),
                basis[:, pl.ds(r0 + 64, 16), :].reshape(MODES * 16, 128),
            ],
            axis=1,
        )
        acc[...] += lax.dot_general(
            lhs, snaps[kb], (((1,), (1,)), ((), ())), preferred_element_type=F32
        )
        return 0

    lax.fori_loop(0, 16, block, 0)

    last = (STEPS // PER % 2) * XB
    for f in range(NF):
        for x in range(CX):
            final_ref[f * CX + x] = state[last + W + x, pl.ds(W * 8 + f, 8, stride=8), :]

    r16 = lax.broadcasted_iota(jnp.int32, (16, 128), 0)
    c16 = lax.broadcasted_iota(jnp.int32, (16, 128), 1)
    diagonal = (c16 % 16 == r16).astype(F32)
    kept = jnp.sum(acc[...].reshape(MODES, 16, 128) * diagonal[None], axis=1)
    kept = jnp.concatenate([kept, jnp.zeros((128 - MODES, 128), F32)], axis=0)
    groups = (lane // 16 == row).astype(F32)
    mine = lax.dot_general(
        groups,
        kept,
        (((1,), (1,)), ((), ())),
        precision=lax.Precision.HIGHEST,
        preferred_element_type=F32,
    )

    def share(slots, peers, rank, n, phase, send, recv):
        copies = []
        for k, (ps, pl_) in enumerate(peers):
            c = pltpu.make_async_remote_copy(
                src_ref=part.at[phase],
                dst_ref=slots.at[k],
                send_sem=send.at[k],
                recv_sem=recv.at[k],
                device_id={"sim": ps, "learn": pl_},
                device_id_type=MESH,
            )
            c.start()
            copies.append(c)
        for c in copies:
            c.wait()

    def total(slots, rank, n, phase):
        out = jnp.zeros((8, 128), F32)
        for r in range(n):
            k = lax.rem(rank - r + n - 1 + n, n)
            mine_now = part[phase]
            other = slots[jnp.minimum(k, n - 2)]
            out = out + jnp.where(rank == r, mine_now, other)
        return out

    part[0] = mine
    share(slots_a, peers_a, rank_a, na, 0, send_a, recv_a)
    part[1] = total(slots_a, rank_a, na, 0)
    share(slots_b, peers_b, rank_b, nb, 1, send_b, recv_b)
    red_ref[...] = total(slots_b, rank_b, nb, 1)


def split3(v):
    hi = v.astype(BF16).astype(F32)
    rest = v - hi
    mi = rest.astype(BF16).astype(F32)
    return hi, mi, rest - mi


def outer_sum(a, b):
    ah, am, al = split3(a)
    bh, bm, bl = split3(b)
    left = jnp.concatenate([ah, ah, am, am, ah, al], axis=0).astype(BF16)
    right = jnp.concatenate([bh, bm, bh, bm, bl, bh], axis=0).astype(BF16)
    return lax.dot_general(left, right, (((0,), (0,)), ((), ())), preferred_element_type=F32)


def tail_kernel(
    rows, red_ref, gram_ref, first_ref, second_ref, state_ref, reduced_ref, pod_ref, rhs_ref, final_ref, sem
):
    keep = pltpu.make_async_copy(state_ref, final_ref, sem)
    keep.start()
    l = lax.axis_index("learn")
    red = red_ref[...]
    row = lax.broadcasted_iota(jnp.int32, (8, 128), 0)
    lane = lax.broadcasted_iota(jnp.int32, (8, 128), 1)
    reduced_ref[...] = red[:, :MODES]
    pod_ref[...] = gram_ref[...] + outer_sum(red, red)[:MODES, :MODES]
    widened = jnp.where(lane == 0, 1.0, pltpu.roll(red, 1, 1))
    changes = jnp.where(row < STEPS - 1, pltpu.roll(red, 7, 0) - red, 0.0)
    feats = []
    for j in range(first_ref.shape[1]):
        one = jnp.broadcast_to(first_ref[l, pl.ds(j, 1), :], (8, 128))
        two = jnp.broadcast_to(second_ref[l, pl.ds(j, 1), :], (8, 128))
        feats.append(
            jnp.take_along_axis(widened, one, axis=1, mode="promise_in_bounds")
            * jnp.take_along_axis(widened, two, axis=1, mode="promise_in_bounds")
        )
    feats = jnp.concatenate(feats, axis=1)
    rhs_ref[...] = outer_sum(changes, feats)[:MODES, :rows]
    keep.wait()


def pair_tables(modes, blocks):
    upper_pairs = np.triu_indices(modes)
    first = np.concatenate([np.zeros(modes), upper_pairs[0] + 1]).astype(np.int32)
    second = np.concatenate([np.arange(modes) + 1, upper_pairs[1] + 1]).astype(np.int32)
    rows = first.shape[0] // blocks
    lines = -(-rows // 128)

    def lay(t):
        t = t.reshape(blocks, rows)
        t = np.pad(t, ((0, 0), (0, lines * 128 - rows)))
        return t.reshape(blocks, lines, 128)

    return rows, lay(first), lay(second)


def solution(mesh):
    sims, learns = mesh.shape["sim"], mesh.shape["learn"]
    dims = ((2, 4, 4), (2, 2)) if (sims, learns) == (32, 4) else ((1, 1, sims), (1, learns))
    (yh_n, z_n, x_n), (yl_n, core_n) = dims
    na, nb = x_n * core_n, yh_n * z_n * yl_n
    rows, first, second = pair_tables(MODES, learns)
    vmem = pl.BlockSpec(memory_space=pltpu.VMEM)
    hbm = pl.BlockSpec(memory_space=pl.ANY)
    n_pieces = len(PIECES)

    def body(fields, diffusivity, stoich, basis, gram_old):
        flat = basis.reshape(MODES, NF * CX * CY, 128)
        final, red = pl.pallas_call(
            functools.partial(steps_kernel, dims),
            out_shape=(
                jax.ShapeDtypeStruct((NF * CX, CY, 128), F32),
                jax.ShapeDtypeStruct((8, 128), F32),
            ),
            in_specs=[hbm] * 4,
            out_specs=(vmem, vmem),
            scratch_shapes=[
                pltpu.VMEM((2 * XB, YB * 8, 128), F32),
                pltpu.VMEM((XB, YB * 8, 128), F32),
                pltpu.VMEM((2 * XB, YB * 8, 128), F32),
                pltpu.VMEM((XB, -(-YB // 8) * 8, 128), F32),
                pltpu.VMEM((16, 128, 256), BF16),
                pltpu.VMEM((MODES, NF * CX * CY, 128), BF16),
                pltpu.VMEM((MODES * 16, 128), F32),
                pltpu.SMEM((NF,), F32),
                pltpu.SMEM((NF,), F32),
                pltpu.VMEM((NF * CX, CY, 128), F32),
                pltpu.SemaphoreType.DMA((3,)),
                pltpu.VMEM((2, 8, 128), F32),
                pltpu.VMEM((max(na - 1, 1), 8, 128), F32),
                pltpu.VMEM((max(nb - 1, 1), 8, 128), F32),
                pltpu.SemaphoreType.DMA,
                pltpu.SemaphoreType.DMA((2, n_pieces)),
                pltpu.SemaphoreType.DMA((2, n_pieces)),
                pltpu.SemaphoreType.DMA((max(na - 1, 1),)),
                pltpu.SemaphoreType.DMA((max(na - 1, 1),)),
                pltpu.SemaphoreType.DMA((max(nb - 1, 1),)),
                pltpu.SemaphoreType.DMA((max(nb - 1, 1),)),
            ],
            compiler_params=pltpu.CompilerParams(
                collective_id=0, has_side_effects=True, vmem_limit_bytes=60 * 1024 * 1024
            ),
            name="steps",
        )(diffusivity, stoich, fields.reshape(NF * CX, CY, 128), flat)
        reduced, pod, rhs, final = pl.pallas_call(
            functools.partial(tail_kernel, rows),
            out_shape=(
                jax.ShapeDtypeStruct((STEPS, MODES), F32),
                jax.ShapeDtypeStruct((MODES, MODES), F32),
                jax.ShapeDtypeStruct((MODES, rows), F32),
                jax.ShapeDtypeStruct((NF * CX, CY, 128), F32),
            ),
            in_specs=[vmem] * 4 + [hbm],
            out_specs=(vmem,) * 3 + (hbm,),
            scratch_shapes=[pltpu.SemaphoreType.DMA],
            compiler_params=pltpu.CompilerParams(vmem_limit_bytes=60 * 1024 * 1024),
            name="tail",
        )(red, gram_old, jnp.asarray(first), jnp.asarray(second), final)
        return final.reshape(NF, CX, CY, 128), reduced.T, pod, rhs.T

    in_specs = (
        P(None, "sim", "learn", None),
        P(),
        P(),
        P(None, None, "sim", "learn", None),
        P(),
    )
    out_specs = (P(None, "sim", "learn", None), P(), P(), P("learn", None))
    return jax.shard_map(body, mesh=mesh, in_specs=in_specs, out_specs=out_specs, check_vma=False)
```

```python
import functools

import jax
import jax.numpy as jnp
import numpy as np
from jax import lax
from jax.experimental import pallas as pl
from jax.experimental.pallas import tpu as pltpu
from jax.sharding import PartitionSpec as P

MESH = pl.DeviceIdType.MESH
STEPS = 8
PER = 4
W = 2 * PER
NF = 8
CX = 8
CY = 8
XB = CX + 2 * W
YB = CY + 2 * W
MODES = 96
F32 = jnp.float32
BF16 = jnp.bfloat16

time_step = 0.1
drift_x = 1.2
drift_y = 1.0
drift_z = 0.3
arrhenius = 2.0
activation = 1.0

DIRS = [(dx, dy) for dx in (-1, 0, 1) for dy in (-1, 0, 1) if (dx, dy) != (0, 0)]

GROUPS = ((1, 2), (3, 4), (5, 6), (7, 8))
NEAR = 2


def pieces():
    out, names = [], {}

    def add(name, *piece):
        names[name] = len(out)
        out.append(piece)

    def along_y(dy, n):
        return (W, W + CY) if dy < 0 else (W + CY - n, W - n)

    for g, (a, b) in enumerate(GROUPS):
        n = b - a + 1
        for dx in (-1, 1):
            sx, tx = (W + a - 1, W + CX + a - 1) if dx < 0 else (W + CX - b, W - b)
            add(("x", g, dx), dx, 0, 0, sx, W, tx, W, n, CY)
        if g == 0:
            for dy in (-1, 1):
                sy, ty = along_y(dy, CY)
                add(("y", dy), 0, dy, 0, W, sy, W, ty, CX, CY)
        rows = min(n, W - a)
        for dx in (-1, 1):
            sx, tx = (W + a - 1, W + CX + a - 1) if dx < 0 else (W + CX - a - rows + 1, W - a - rows + 1)
            for dy in (-1, 1):
                sy, ty = along_y(dy, W - a)
                add(("d", g, dx, dy), dx, dy, 0, sx, sy, tx, ty, rows, W - a)
    direct = len(out)
    for g, (a, b) in enumerate(GROUPS[:NEAR]):
        for side in (-1, 1):
            x = W - b if side < 0 else W + CX + a - 1
            for dy in (-1, 1):
                sy, ty = along_y(dy, W - a)
                add(("f", g, side, dy), 0, dy, side, x, sy, x, ty, b - a + 1, W - a)
    return out, names, direct


PIECES, NAMES, DIRECT = pieces()
FAR = [NAMES["d", g, dx, dy] for g in range(NEAR) for dx in (-1, 1) for dy in (-1, 1)]


def steps_kernel(
    dims,
    diff_hbm,
    stoich_hbm,
    fields_hbm,
    basis_ref,
    final_ref,
    red_ref,
    state,
    mid,
    later,
    rate,
    snaps,
    basis,
    acc,
    diff_ref,
    stoich_ref,
    fields_ref,
    in_sem,
    part,
    slots_a,
    slots_b,
    basis_sem,
    send_sem,
    recv_sem,
    send_a,
    recv_a,
    send_b,
    recv_b,
):
    (yh_n, z_n, x_n), (yl_n, core_n) = dims
    sims, learns = yh_n * z_n * x_n, yl_n * core_n
    s = lax.axis_index("sim")
    l = lax.axis_index("learn")

    fetch = pltpu.make_async_copy(basis_ref, basis, basis_sem)
    loads = [
        pltpu.make_async_copy(a, b, in_sem.at[i])
        for i, (a, b) in enumerate(
            ((fields_hbm, fields_ref), (diff_hbm, diff_ref), (stoich_hbm, stoich_ref))
        )
    ]
    for c in loads:
        c.start()
    fetch.start()

    for par in range(2):
        for edge, x in ((s == 0, par * XB), (s == lax.axis_size("sim") - 1, par * XB + W + CX)):

            @pl.when(edge)
            def _(x=x):
                state[pl.ds(x, W)] = jnp.zeros((W, YB * 8, 128), F32)

        for edge, y in ((l == 0, 0), (l == lax.axis_size("learn") - 1, W + CY)):

            @pl.when(edge)
            def _(par=par, y=y):
                state[pl.ds(par * XB, XB), pl.ds(y * 8, W * 8), :] = jnp.zeros((XB, W * 8, 128), F32)

    x_me = s % x_n
    z_me = (s // x_n) % z_n
    yh_me = s // (x_n * z_n)
    core_me = l % core_n
    yl_me = l // core_n

    peers_a = []
    na = x_n * core_n
    rank_a = x_me * core_n + core_me
    for k in range(1, na):
        r = (rank_a + k) % na
        peers_a.append(((s - x_me) + r // core_n, (l - core_me) + r % core_n))
    peers_b = []
    nb = yh_n * z_n * yl_n
    rank_b = (yh_me * z_n + z_me) * yl_n + yl_me
    for k in range(1, nb):
        r = (rank_b + k) % nb
        yz = r // yl_n
        peers_b.append((yz * x_n + x_me, (r % yl_n) * core_n + core_me))

    def there(dx, dy):
        ok = None
        for d, me, n in ((dx, s, sims), (dy, l, learns)):
            if d == 0:
                continue
            c = me > 0 if d < 0 else me < n - 1
            ok = c if ok is None else ok & c
        return ok

    def on_chip(dy, arriving):
        return core_me == (0 if (dy > 0) != arriving else 1)

    barrier = pltpu.get_barrier_semaphore()
    count = jnp.int32(len(peers_a) + len(peers_b))
    for dx, dy in DIRS:
        ok = there(dx, dy)
        count = count + ok.astype(jnp.int32)

        @pl.when(ok)
        def _(dx=dx, dy=dy):
            pl.semaphore_signal(
                barrier, inc=1, device_id={"sim": s + dx, "learn": l + dy}, device_id_type=MESH
            )

    for ps, pl_ in peers_a + peers_b:
        pl.semaphore_signal(barrier, inc=1, device_id={"sim": ps, "learn": pl_}, device_id_type=MESH)

    for c in loads:
        c.wait()

    for f in range(NF):
        for x in range(CX):
            state[W + x, pl.ds(W * 8 + f, 8, stride=8), :] = fields_ref[f * CX + x]

    row = lax.broadcasted_iota(jnp.int32, (8, 128), 0)
    lane = lax.broadcasted_iota(jnp.int32, (8, 128), 1)
    diff = jnp.zeros((8, 128), F32)
    sto = jnp.zeros((8, 128), F32)
    for f in range(NF):
        diff = jnp.where(row == f, diff_ref[f], diff)
        sto = jnp.where(row == f, stoich_ref[f], sto)

    def coefs(scale, keep):
        upper = jnp.where(lane < 127, scale * (diff - 0.5 * drift_z), 0.0)
        lower = jnp.where(lane > 0, scale * (diff + 0.5 * drift_z), 0.0)
        return (
            keep - (6.0 * scale) * diff,
            scale * (diff - 0.5 * drift_x),
            scale * (diff + 0.5 * drift_x),
            scale * (diff - 0.5 * drift_y),
            scale * (diff + 0.5 * drift_y),
            upper,
            lower,
            (scale * arrhenius) * sto,
        )

    coefs_1 = coefs(time_step, 1.0)
    coefs_2 = coefs(0.5 * time_step, 0.5)

    x_low = jnp.where(s > 0, 1.0, 0.0).astype(F32)
    x_high = jnp.where(s < sims - 1, 1.0, 0.0).astype(F32)
    y_low = jnp.where(l > 0, 1.0, 0.0).astype(F32)
    y_high = jnp.where(l < learns - 1, 1.0, 0.0).astype(F32)

    def beyond(x):
        return max(W - x, x - (W + CX - 1))

    def reach(s_, x):
        e = W - s_ - max(beyond(x), 0)
        return W - e, W + CY + e

    def rates(s_, src, base, x):
        y0, y1 = reach(s_, x)
        for y in sorted({min(y, y1 - 8) for y in range(y0, y1, 8)}):
            u0 = src[base + x, pl.ds(y * 8, 8, stride=8), :]
            u1 = src[base + x, pl.ds(y * 8 + 1, 8, stride=8), :]
            u7 = src[base + x, pl.ds(y * 8 + 7, 8, stride=8), :]
            rate[(s_ - 1) * XB + x, pl.ds(y, 8), :] = (
                jnp.tanh(u0) * jnp.tanh(u1) * jnp.exp(-activation / (1.0 + u7 * u7))
            )

    def cells(ref, x, y, n):
        return ref[x, pl.ds(y * 8, n * 8), :].reshape(n, 8, 128)

    def line(s_, src, base, dst, dbase, x, cs, old=None, obase=0):
        c_c, c_e, c_w, c_n, c_s, c_u, c_l, c_r = (c[None] for c in cs)
        y0, y1 = reach(s_, x)
        ends = sorted({y0, y1} | {y for y in (W, W + CY) if y0 < y < y1})
        for y, end in zip(ends[:-1], ends[1:]):
            n = end - y
            c = cells(src, base + x, y, n)
            q = jnp.stack(
                [
                    jnp.broadcast_to(rate[(s_ - 1) * XB + x, pl.ds(y + j, 1), :], (8, 128))
                    for j in range(n)
                ]
            )
            v = c_c * c + c_e * cells(src, base + x + 1, y, n)
            v = v + (c_w * cells(src, base + x - 1, y, n) + c_n * cells(src, base + x, y + 1, n))
            v = v + (c_s * cells(src, base + x, y - 1, n) + c_r * q)
            v = v + (c_u * pltpu.roll(c, 127, 2) + c_l * pltpu.roll(c, 1, 2))
            if old is not None:
                v = v + 0.5 * cells(old, obase + x, y, n)
            masks = []
            if x < W:
                masks.append(x_low)
            if x >= W + CX:
                masks.append(x_high)
            if y < W:
                masks.append(y_low)
            if y >= W + CY:
                masks.append(y_high)
            if masks:
                v = v * functools.reduce(lambda a, b: a * b, masks)
            dst[dbase + x, pl.ds(y * 8, n * 8), :] = v.reshape(n * 8, 128)

    def snapshot(src, base, t):
        for fp in range(NF // 2):
            for xp in range(CX // 2):
                halves = []
                for f in (2 * fp, 2 * fp + 1):
                    a = src[base + W + 2 * xp, pl.ds(W * 8 + f, 8, stride=8), :]
                    b = src[base + W + 2 * xp + 1, pl.ds(W * 8 + f, 8, stride=8), :]
                    halves.append(jnp.concatenate([a, b], axis=0))
                tile = jnp.concatenate(halves, axis=1).astype(BF16)
                snaps[fp * 4 + xp, pl.ds(pl.multiple_of(t * 16, 16), 16), :] = tile

    def copy(par, k):
        dx, dy, _, sx, sy, tx, ty, nx, ny = PIECES[k]
        return pltpu.make_async_remote_copy(
            src_ref=state.at[pl.ds(par * XB + sx, nx), pl.ds(sy * 8, ny * 8), :],
            dst_ref=state.at[pl.ds(par * XB + tx, nx), pl.ds(ty * 8, ny * 8), :],
            send_sem=send_sem.at[par, k],
            recv_sem=recv_sem.at[par, k],
            device_id={"sim": s + dx, "learn": l + dy},
            device_id_type=MESH,
        )

    pl.semaphore_wait(barrier, count)

    def window(e, _):
        par = lax.rem(e, 2)
        base = par * XB
        nxt = (1 - par) * XB

        def each(chosen, act, arriving):
            for k in chosen:
                dx, dy, side = PIECES[k][:3]
                ok = there(-dx, -dy) if arriving else there(dx, dy)
                if side:
                    ok = ok & there(side, 0) & on_chip(dy, arriving)
                if k in FAR:
                    ok = ok & ~on_chip(dy, arriving)

                @pl.when(ok)
                def _(k=k):
                    act(copy(par, k))

        def send(chosen):
            each(chosen, lambda c: c.start(), False)

        def arrive(*names):
            each([NAMES[n] for n in names], lambda c: c.wait_recv(), True)

        def held(s_):
            if s_ % 2:
                return mid, 0
            if s_ in (0, W):
                return state, (base if s_ == 0 else nxt)
            return later, (s_ // 2 % 2) * XB

        def level(i):
            todo = []
            for s_ in range(1, W + 1):
                for x in range(W - (W - s_), W + CX + (W - s_)):
                    need = max(s_ + beyond(x), 0)
                    if need == i:
                        todo.append((s_, x))
            if i > 0:
                for s_, x in todo:
                    rates(s_, *held(s_ - 1), x)
            done = 0
            for s_, x in todo:
                if i == 0 and s_ != done:
                    for t_, z in todo:
                        if t_ == s_:
                            rates(s_, *held(s_ - 1), z)
                    done = s_
                if s_ % 2:
                    line(s_, *held(s_ - 1), *held(s_), x, coefs_1)
                else:
                    line(s_, *held(s_ - 1), *held(s_), x, coefs_2, *held(s_ - 2))

        pairs = [(a, b) for a in (-1, 1) for b in (-1, 1)]
        send(range(DIRECT))
        arrive(("y", -1), ("y", 1))
        level(0)
        for g in range(NEAR):
            for dx in (-1, 1):
                arrive(("x", g, dx))
                send([NAMES["f", g, -dx, dy] for dy in (-1, 1)])
        for g, (a, b) in enumerate(GROUPS):
            if g < NEAR:
                arrive(*[("f", g, side, dy) for side, dy in pairs])
                arrive(*[("d", g, dx, dy) for dx, dy in pairs])
            else:
                arrive(("x", g, -1), ("x", g, 1), *[("d", g, dx, dy) for dx, dy in pairs])
            for i in range(a, b + 1):
                level(i)
            snapshot(*held(b), e * PER + g)
        each(range(len(PIECES)), lambda c: c.wait_send(), False)
        return 0

    lax.fori_loop(0, STEPS // PER, window, 0)

    last = (STEPS // PER % 2) * XB
    for f in range(NF):
        for x in range(CX):
            fields_ref[f * CX + x] = state[last + W + x, pl.ds(W * 8 + f, 8, stride=8), :]
    keep = pltpu.make_async_copy(fields_ref, final_ref, in_sem.at[0])
    keep.start()

    fetch.wait()
    left, right = [], []
    for fp in range(NF // 2):
        for xp in range(CX // 2):
            for f in (2 * fp, 2 * fp + 1):
                rows = basis[:, pl.ds(f * CX * CY + xp * 16, 16), :]
                left.append(rows.reshape(MODES * 16, 128))
            right.append(snaps[fp * 4 + xp])
    acc[...] = lax.dot_general(
        jnp.concatenate(left, axis=1),
        jnp.concatenate(right, axis=1),
        (((1,), (1,)), ((), ())),
        preferred_element_type=F32,
    )

    r16 = lax.broadcasted_iota(jnp.int32, (16, 128), 0)
    c16 = lax.broadcasted_iota(jnp.int32, (16, 128), 1)
    diagonal = (c16 % 16 == r16).astype(F32)
    kept = jnp.sum(acc[...].reshape(MODES, 16, 128) * diagonal[None], axis=1)
    kept = jnp.concatenate([kept, jnp.zeros((128 - MODES, 128), F32)], axis=0)
    groups = (lane // 16 == row).astype(F32)
    mine = lax.dot_general(
        groups,
        kept,
        (((1,), (1,)), ((), ())),
        precision=lax.Precision.HIGHEST,
        preferred_element_type=F32,
    )

    def share(slots, peers, rank, n, phase, send, recv):
        copies = []
        for k, (ps, pl_) in enumerate(peers):
            c = pltpu.make_async_remote_copy(
                src_ref=part.at[phase],
                dst_ref=slots.at[k],
                send_sem=send.at[k],
                recv_sem=recv.at[k],
                device_id={"sim": ps, "learn": pl_},
                device_id_type=MESH,
            )
            c.start()
            copies.append(c)
        for c in copies:
            c.wait()

    def total(slots, rank, n, phase):
        out = jnp.zeros((8, 128), F32)
        for r in range(n):
            k = lax.rem(rank - r + n - 1 + n, n)
            mine_now = part[phase]
            other = slots[jnp.minimum(k, n - 2)]
            out = out + jnp.where(rank == r, mine_now, other)
        return out

    part[0] = mine
    share(slots_a, peers_a, rank_a, na, 0, send_a, recv_a)
    part[1] = total(slots_a, rank_a, na, 0)
    share(slots_b, peers_b, rank_b, nb, 1, send_b, recv_b)
    red_ref[...] = total(slots_b, rank_b, nb, 1)
    keep.wait()


def split3(v):
    hi = v.astype(BF16).astype(F32)
    rest = v - hi
    mi = rest.astype(BF16).astype(F32)
    return hi, mi, rest - mi


def outer_sum(a, b):
    ah, am, al = split3(a)
    bh, bm, bl = split3(b)
    left = jnp.concatenate([ah, ah, am, am, ah, al], axis=0).astype(BF16)
    right = jnp.concatenate([bh, bm, bh, bm, bl, bh], axis=0).astype(BF16)
    return lax.dot_general(left, right, (((0,), (0,)), ((), ())), preferred_element_type=F32)


def tail_kernel(
    rows, red_ref, gram_ref, first_ref, second_ref, state_ref, reduced_ref, pod_ref, rhs_ref, final_ref, held, sem
):
    bring = pltpu.make_async_copy(state_ref, held, sem.at[0])
    bring.start()
    keep = pltpu.make_async_copy(held, final_ref, sem.at[1])
    l = lax.axis_index("learn")
    red = red_ref[...]
    row = lax.broadcasted_iota(jnp.int32, (8, 128), 0)
    lane = lax.broadcasted_iota(jnp.int32, (8, 128), 1)
    bring.wait()
    keep.start()
    reduced_ref[...] = red[:, :MODES]
    pod_ref[...] = gram_ref[...] + outer_sum(red, red)[:MODES, :MODES]
    widened = jnp.where(lane == 0, 1.0, pltpu.roll(red, 1, 1))
    changes = jnp.where(row < STEPS - 1, pltpu.roll(red, 7, 0) - red, 0.0)
    feats = []
    for j in range(first_ref.shape[1]):
        one = jnp.broadcast_to(first_ref[l, pl.ds(j, 1), :], (8, 128))
        two = jnp.broadcast_to(second_ref[l, pl.ds(j, 1), :], (8, 128))
        feats.append(
            jnp.take_along_axis(widened, one, axis=1, mode="promise_in_bounds")
            * jnp.take_along_axis(widened, two, axis=1, mode="promise_in_bounds")
        )
    feats = jnp.concatenate(feats, axis=1)
    rhs_ref[...] = outer_sum(changes, feats)[:MODES, :rows]
    keep.wait()


def pair_tables(modes, blocks):
    upper_pairs = np.triu_indices(modes)
    first = np.concatenate([np.zeros(modes), upper_pairs[0] + 1]).astype(np.int32)
    second = np.concatenate([np.arange(modes) + 1, upper_pairs[1] + 1]).astype(np.int32)
    rows = first.shape[0] // blocks
    lines = -(-rows // 128)

    def lay(t):
        t = t.reshape(blocks, rows)
        t = np.pad(t, ((0, 0), (0, lines * 128 - rows)))
        return t.reshape(blocks, lines, 128)

    return rows, lay(first), lay(second)


def solution(mesh):
    sims, learns = mesh.shape["sim"], mesh.shape["learn"]
    dims = ((2, 4, 4), (2, 2)) if (sims, learns) == (32, 4) else ((1, 1, sims), (1, learns))
    (yh_n, z_n, x_n), (yl_n, core_n) = dims
    na, nb = x_n * core_n, yh_n * z_n * yl_n
    rows, first, second = pair_tables(MODES, learns)
    vmem = pl.BlockSpec(memory_space=pltpu.VMEM)
    hbm = pl.BlockSpec(memory_space=pl.ANY)
    n_pieces = len(PIECES)

    def body(fields, diffusivity, stoich, basis, gram_old):
        flat = basis.reshape(MODES, NF * CX * CY, 128)
        final, red = pl.pallas_call(
            functools.partial(steps_kernel, dims),
            out_shape=(
                jax.ShapeDtypeStruct((NF * CX, CY, 128), F32),
                jax.ShapeDtypeStruct((8, 128), F32),
            ),
            in_specs=[hbm] * 4,
            out_specs=(hbm, vmem),
            scratch_shapes=[
                pltpu.VMEM((2 * XB, YB * 8, 128), F32),
                pltpu.VMEM((XB, YB * 8, 128), F32),
                pltpu.VMEM((2 * XB, YB * 8, 128), F32),
                pltpu.VMEM((W * XB, -(-YB // 8) * 8, 128), F32),
                pltpu.VMEM((16, 128, 256), BF16),
                pltpu.VMEM((MODES, NF * CX * CY, 128), BF16),
                pltpu.VMEM((MODES * 16, 128), F32),
                pltpu.SMEM((NF,), F32),
                pltpu.SMEM((NF,), F32),
                pltpu.VMEM((NF * CX, CY, 128), F32),
                pltpu.SemaphoreType.DMA((3,)),
                pltpu.VMEM((2, 8, 128), F32),
                pltpu.VMEM((max(na - 1, 1), 8, 128), F32),
                pltpu.VMEM((max(nb - 1, 1), 8, 128), F32),
                pltpu.SemaphoreType.DMA,
                pltpu.SemaphoreType.DMA((2, n_pieces)),
                pltpu.SemaphoreType.DMA((2, n_pieces)),
                pltpu.SemaphoreType.DMA((max(na - 1, 1),)),
                pltpu.SemaphoreType.DMA((max(na - 1, 1),)),
                pltpu.SemaphoreType.DMA((max(nb - 1, 1),)),
                pltpu.SemaphoreType.DMA((max(nb - 1, 1),)),
            ],
            compiler_params=pltpu.CompilerParams(
                collective_id=0, has_side_effects=True, vmem_limit_bytes=60 * 1024 * 1024
            ),
            name="steps",
        )(diffusivity, stoich, fields.reshape(NF * CX, CY, 128), flat)
        reduced, pod, rhs, final = pl.pallas_call(
            functools.partial(tail_kernel, rows),
            out_shape=(
                jax.ShapeDtypeStruct((STEPS, MODES), F32),
                jax.ShapeDtypeStruct((MODES, MODES), F32),
                jax.ShapeDtypeStruct((MODES, rows), F32),
                jax.ShapeDtypeStruct((NF * CX, CY, 128), F32),
            ),
            in_specs=[vmem] * 4 + [hbm],
            out_specs=(vmem,) * 3 + (hbm,),
            scratch_shapes=[pltpu.VMEM((NF * CX, CY, 128), F32), pltpu.SemaphoreType.DMA((2,))],
            compiler_params=pltpu.CompilerParams(vmem_limit_bytes=60 * 1024 * 1024),
            name="tail",
        )(red, gram_old, jnp.asarray(first), jnp.asarray(second), final)
        return final.reshape(NF, CX, CY, 128), reduced.T, pod, rhs.T

    in_specs = (
        P(None, "sim", "learn", None),
        P(),
        P(),
        P(None, None, "sim", "learn", None),
        P(),
    )
    out_specs = (P(None, "sim", "learn", None), P(), P(), P("learn", None))
    return jax.shard_map(body, mesh=mesh, in_specs=in_specs, out_specs=out_specs, check_vma=False)
```

```python
import functools

import jax
import jax.numpy as jnp
import numpy as np
from jax import lax
from jax.experimental import pallas as pl
from jax.experimental.pallas import tpu as pltpu
from jax.sharding import PartitionSpec as P

MESH = pl.DeviceIdType.MESH
STEPS = 8
PER = 4
W = 2 * PER
NF = 8
CX = 8
CY = 8
XB = CX + 2 * W
YB = CY + 2 * W
MODES = 96
F32 = jnp.float32
BF16 = jnp.bfloat16

time_step = 0.1
drift_x = 1.2
drift_y = 1.0
drift_z = 0.3
arrhenius = 2.0
activation = 1.0

DIRS = [(dx, dy) for dx in (-1, 0, 1) for dy in (-1, 0, 1) if (dx, dy) != (0, 0)]

GROUPS = ((1, 2), (3, 4), (5, 6), (7, 8))
NEAR = 2


def pieces():
    out, names = [], {}

    def add(name, *piece):
        names[name] = len(out)
        out.append(piece)

    def along_y(dy, n):
        return (W, W + CY) if dy < 0 else (W + CY - n, W - n)

    for g, (a, b) in enumerate(GROUPS):
        n = b - a + 1
        for dx in (-1, 1):
            sx, tx = (W + a - 1, W + CX + a - 1) if dx < 0 else (W + CX - b, W - b)
            add(("x", g, dx), dx, 0, 0, sx, W, tx, W, n, CY)
        if g == 0:
            for dy in (-1, 1):
                sy, ty = along_y(dy, CY)
                add(("y", dy), 0, dy, 0, W, sy, W, ty, CX, CY)
        rows = min(n, W - a)
        for dx in (-1, 1):
            sx, tx = (W + a - 1, W + CX + a - 1) if dx < 0 else (W + CX - a - rows + 1, W - a - rows + 1)
            for dy in (-1, 1):
                sy, ty = along_y(dy, W - a)
                add(("d", g, dx, dy), dx, dy, 0, sx, sy, tx, ty, rows, W - a)
    direct = len(out)
    for g, (a, b) in enumerate(GROUPS[:NEAR]):
        for side in (-1, 1):
            x = W - b if side < 0 else W + CX + a - 1
            for dy in (-1, 1):
                sy, ty = along_y(dy, W - a)
                add(("f", g, side, dy), 0, dy, side, x, sy, x, ty, b - a + 1, W - a)
    return out, names, direct


PIECES, NAMES, DIRECT = pieces()
FAR = [NAMES["d", g, dx, dy] for g in range(NEAR) for dx in (-1, 1) for dy in (-1, 1)]


def steps_kernel(
    dims,
    diff_hbm,
    stoich_hbm,
    fields_hbm,
    basis_ref,
    final_ref,
    red_ref,
    state,
    mid,
    later,
    rate,
    snaps,
    basis,
    acc,
    diff_ref,
    stoich_ref,
    fields_ref,
    in_sem,
    part,
    slots_a,
    slots_b,
    basis_sem,
    send_sem,
    recv_sem,
    send_a,
    recv_a,
    send_b,
    recv_b,
):
    (yh_n, z_n, x_n), (yl_n, core_n) = dims
    sims, learns = yh_n * z_n * x_n, yl_n * core_n
    s = lax.axis_index("sim")
    l = lax.axis_index("learn")

    fetch = pltpu.make_async_copy(basis_ref, basis, basis_sem)
    loads = [
        pltpu.make_async_copy(a, b, in_sem.at[i])
        for i, (a, b) in enumerate(
            ((fields_hbm, fields_ref), (diff_hbm, diff_ref), (stoich_hbm, stoich_ref))
        )
    ]
    for c in loads:
        c.start()
    fetch.start()

    for par in range(2):
        for edge, x in ((s == 0, par * XB), (s == lax.axis_size("sim") - 1, par * XB + W + CX)):

            @pl.when(edge)
            def _(x=x):
                state[pl.ds(x, W)] = jnp.zeros((W, YB * 8, 128), F32)

        for edge, y in ((l == 0, 0), (l == lax.axis_size("learn") - 1, W + CY)):

            @pl.when(edge)
            def _(par=par, y=y):
                state[pl.ds(par * XB, XB), pl.ds(y * 8, W * 8), :] = jnp.zeros((XB, W * 8, 128), F32)

    x_me = s % x_n
    z_me = (s // x_n) % z_n
    yh_me = s // (x_n * z_n)
    core_me = l % core_n
    yl_me = l // core_n

    peers_a = []
    na = x_n * core_n
    rank_a = x_me * core_n + core_me
    for k in range(1, na):
        r = (rank_a + k) % na
        peers_a.append(((s - x_me) + r // core_n, (l - core_me) + r % core_n))
    peers_b = []
    nb = yh_n * z_n * yl_n
    rank_b = (yh_me * z_n + z_me) * yl_n + yl_me
    for k in range(1, nb):
        r = (rank_b + k) % nb
        yz = r // yl_n
        peers_b.append((yz * x_n + x_me, (r % yl_n) * core_n + core_me))

    def there(dx, dy):
        ok = None
        for d, me, n in ((dx, s, sims), (dy, l, learns)):
            if d == 0:
                continue
            c = me > 0 if d < 0 else me < n - 1
            ok = c if ok is None else ok & c
        return ok

    def on_chip(dy, arriving):
        return core_me == (0 if (dy > 0) != arriving else 1)

    barrier = pltpu.get_barrier_semaphore()
    count = jnp.int32(len(peers_a) + len(peers_b))
    for dx, dy in DIRS:
        ok = there(dx, dy)
        count = count + ok.astype(jnp.int32)

        @pl.when(ok)
        def _(dx=dx, dy=dy):
            pl.semaphore_signal(
                barrier, inc=1, device_id={"sim": s + dx, "learn": l + dy}, device_id_type=MESH
            )

    for ps, pl_ in peers_a + peers_b:
        pl.semaphore_signal(barrier, inc=1, device_id={"sim": ps, "learn": pl_}, device_id_type=MESH)

    for c in loads:
        c.wait()

    for f in range(NF):
        for x in range(CX):
            state[W + x, pl.ds(W * 8 + f, 8, stride=8), :] = fields_ref[f * CX + x]

    row = lax.broadcasted_iota(jnp.int32, (8, 128), 0)
    lane = lax.broadcasted_iota(jnp.int32, (8, 128), 1)
    diff = jnp.zeros((8, 128), F32)
    sto = jnp.zeros((8, 128), F32)
    for f in range(NF):
        diff = jnp.where(row == f, diff_ref[f], diff)
        sto = jnp.where(row == f, stoich_ref[f], sto)

    def coefs(scale, keep):
        upper = jnp.where(lane < 127, scale * (diff - 0.5 * drift_z), 0.0)
        lower = jnp.where(lane > 0, scale * (diff + 0.5 * drift_z), 0.0)
        return (
            keep - (6.0 * scale) * diff,
            scale * (diff - 0.5 * drift_x),
            scale * (diff + 0.5 * drift_x),
            scale * (diff - 0.5 * drift_y),
            scale * (diff + 0.5 * drift_y),
            upper,
            lower,
            (scale * arrhenius) * sto,
        )

    coefs_1 = coefs(time_step, 1.0)
    coefs_2 = coefs(0.5 * time_step, 0.5)

    x_low = jnp.where(s > 0, 1.0, 0.0).astype(F32)
    x_high = jnp.where(s < sims - 1, 1.0, 0.0).astype(F32)
    y_low = jnp.where(l > 0, 1.0, 0.0).astype(F32)
    y_high = jnp.where(l < learns - 1, 1.0, 0.0).astype(F32)

    def beyond(x):
        return max(W - x, x - (W + CX - 1))

    def reach(s_, x):
        e = W - s_ - max(beyond(x), 0)
        return W - e, W + CY + e

    def rates(s_, src, base, x):
        y0, y1 = reach(s_, x)
        for y in sorted({min(y, y1 - 8) for y in range(y0, y1, 8)}):
            u0 = src[base + x, pl.ds(y * 8, 8, stride=8), :]
            u1 = src[base + x, pl.ds(y * 8 + 1, 8, stride=8), :]
            u7 = src[base + x, pl.ds(y * 8 + 7, 8, stride=8), :]
            rate[(s_ - 1) * XB + x, pl.ds(y, 8), :] = (
                jnp.tanh(u0) * jnp.tanh(u1) * jnp.exp(-activation / (1.0 + u7 * u7))
            )

    def cells(ref, x, y, n):
        return ref[x, pl.ds(y * 8, n * 8), :].reshape(n, 8, 128)

    def line(s_, src, base, dst, dbase, x, cs, old=None, obase=0):
        c_c, c_e, c_w, c_n, c_s, c_u, c_l, c_r = (c[None] for c in cs)
        y0, y1 = reach(s_, x)
        ends = sorted({y0, y1} | {y for y in (W, W + CY) if y0 < y < y1})
        for y, end in zip(ends[:-1], ends[1:]):
            n = end - y
            c = cells(src, base + x, y, n)
            q = jnp.stack(
                [
                    jnp.broadcast_to(rate[(s_ - 1) * XB + x, pl.ds(y + j, 1), :], (8, 128))
                    for j in range(n)
                ]
            )
            v = c_c * c + c_e * cells(src, base + x + 1, y, n)
            v = v + (c_w * cells(src, base + x - 1, y, n) + c_n * cells(src, base + x, y + 1, n))
            v = v + (c_s * cells(src, base + x, y - 1, n) + c_r * q)
            v = v + (c_u * pltpu.roll(c, 127, 2) + c_l * pltpu.roll(c, 1, 2))
            if old is not None:
                v = v + 0.5 * cells(old, obase + x, y, n)
            masks = []
            if x < W:
                masks.append(x_low)
            if x >= W + CX:
                masks.append(x_high)
            if y < W:
                masks.append(y_low)
            if y >= W + CY:
                masks.append(y_high)
            if masks:
                v = v * functools.reduce(lambda a, b: a * b, masks)
            dst[dbase + x, pl.ds(y * 8, n * 8), :] = v.reshape(n * 8, 128)

    def snapshot(src, base, t):
        for fp in range(NF // 2):
            for xp in range(CX // 2):
                halves = []
                for f in (2 * fp, 2 * fp + 1):
                    a = src[base + W + 2 * xp, pl.ds(W * 8 + f, 8, stride=8), :]
                    b = src[base + W + 2 * xp + 1, pl.ds(W * 8 + f, 8, stride=8), :]
                    halves.append(jnp.concatenate([a, b], axis=0))
                tile = jnp.concatenate(halves, axis=1).astype(BF16)
                snaps[fp * 4 + xp, pl.ds(pl.multiple_of(t * 16, 16), 16), :] = tile

    def copy(par, k):
        dx, dy, _, sx, sy, tx, ty, nx, ny = PIECES[k]
        return pltpu.make_async_remote_copy(
            src_ref=state.at[pl.ds(par * XB + sx, nx), pl.ds(sy * 8, ny * 8), :],
            dst_ref=state.at[pl.ds(par * XB + tx, nx), pl.ds(ty * 8, ny * 8), :],
            send_sem=send_sem.at[par, k],
            recv_sem=recv_sem.at[par, k],
            device_id={"sim": s + dx, "learn": l + dy},
            device_id_type=MESH,
        )

    pl.semaphore_wait(barrier, count)

    def window(e, _):
        par = lax.rem(e, 2)
        base = par * XB
        nxt = (1 - par) * XB

        def each(chosen, act, arriving):
            for k in chosen:
                dx, dy, side = PIECES[k][:3]
                ok = there(-dx, -dy) if arriving else there(dx, dy)
                if side:
                    ok = ok & there(side, 0) & on_chip(dy, arriving)
                if k in FAR:
                    ok = ok & ~on_chip(dy, arriving)

                @pl.when(ok)
                def _(k=k):
                    act(copy(par, k))

        def send(chosen):
            each(chosen, lambda c: c.start(), False)

        def arrive(*names):
            each([NAMES[n] for n in names], lambda c: c.wait_recv(), True)

        def held(s_):
            if s_ % 2:
                return mid, 0
            if s_ in (0, W):
                return state, (base if s_ == 0 else nxt)
            return later, (s_ // 2 % 2) * XB

        def level(i):
            todo = []
            for s_ in range(1, W + 1):
                for x in range(W - (W - s_), W + CX + (W - s_)):
                    need = max(s_ + beyond(x), 0)
                    if need == i:
                        todo.append((s_, x))
            if i > 0:
                for s_, x in todo:
                    rates(s_, *held(s_ - 1), x)
            done = 0
            for s_, x in todo:
                if i == 0 and s_ != done:
                    for t_, z in todo:
                        if t_ == s_:
                            rates(s_, *held(s_ - 1), z)
                    done = s_
                if s_ % 2:
                    line(s_, *held(s_ - 1), *held(s_), x, coefs_1)
                else:
                    line(s_, *held(s_ - 1), *held(s_), x, coefs_2, *held(s_ - 2))

        pairs = [(a, b) for a in (-1, 1) for b in (-1, 1)]
        send(range(DIRECT))
        arrive(("y", -1), ("y", 1))
        level(0)
        for g in range(NEAR):
            for dx in (-1, 1):
                arrive(("x", g, dx))
                send([NAMES["f", g, -dx, dy] for dy in (-1, 1)])
        for g, (a, b) in enumerate(GROUPS):
            if g < NEAR:
                arrive(*[("f", g, side, dy) for side, dy in pairs])
                arrive(*[("d", g, dx, dy) for dx, dy in pairs])
            else:
                arrive(("x", g, -1), ("x", g, 1), *[("d", g, dx, dy) for dx, dy in pairs])
            for i in range(a, b + 1):
                level(i)
                if i % 2 == 0:
                    snapshot(*held(i), e * PER + i // 2 - 1)
        each(range(len(PIECES)), lambda c: c.wait_send(), False)
        return 0

    lax.fori_loop(0, STEPS // PER, window, 0)

    last = (STEPS // PER % 2) * XB
    for f in range(NF):
        for x in range(CX):
            fields_ref[f * CX + x] = state[last + W + x, pl.ds(W * 8 + f, 8, stride=8), :]
    keep = pltpu.make_async_copy(fields_ref, final_ref, in_sem.at[0])
    keep.start()

    fetch.wait()
    left, right = [], []
    for fp in range(NF // 2):
        for xp in range(CX // 2):
            for f in (2 * fp, 2 * fp + 1):
                rows = basis[:, pl.ds(f * CX * CY + xp * 16, 16), :]
                left.append(rows.reshape(MODES * 16, 128))
            right.append(snaps[fp * 4 + xp])
    acc[...] = lax.dot_general(
        jnp.concatenate(left, axis=1),
        jnp.concatenate(right, axis=1),
        (((1,), (1,)), ((), ())),
        preferred_element_type=F32,
    )

    r16 = lax.broadcasted_iota(jnp.int32, (16, 128), 0)
    c16 = lax.broadcasted_iota(jnp.int32, (16, 128), 1)
    diagonal = (c16 % 16 == r16).astype(F32)
    kept = jnp.sum(acc[...].reshape(MODES, 16, 128) * diagonal[None], axis=1)
    kept = jnp.concatenate([kept, jnp.zeros((128 - MODES, 128), F32)], axis=0)
    groups = (lane // 16 == row).astype(F32)
    mine = lax.dot_general(
        groups,
        kept,
        (((1,), (1,)), ((), ())),
        precision=lax.Precision.HIGHEST,
        preferred_element_type=F32,
    )

    def share(slots, peers, rank, n, phase, send, recv):
        copies = []
        for k, (ps, pl_) in enumerate(peers):
            c = pltpu.make_async_remote_copy(
                src_ref=part.at[phase],
                dst_ref=slots.at[k],
                send_sem=send.at[k],
                recv_sem=recv.at[k],
                device_id={"sim": ps, "learn": pl_},
                device_id_type=MESH,
            )
            c.start()
            copies.append(c)
        for c in copies:
            c.wait()

    def total(slots, rank, n, phase):
        out = jnp.zeros((8, 128), F32)
        for r in range(n):
            k = lax.rem(rank - r + n - 1 + n, n)
            mine_now = part[phase]
            other = slots[jnp.minimum(k, n - 2)]
            out = out + jnp.where(rank == r, mine_now, other)
        return out

    part[0] = mine
    share(slots_a, peers_a, rank_a, na, 0, send_a, recv_a)
    part[1] = total(slots_a, rank_a, na, 0)
    share(slots_b, peers_b, rank_b, nb, 1, send_b, recv_b)
    red_ref[...] = total(slots_b, rank_b, nb, 1)
    keep.wait()


def split3(v):
    hi = v.astype(BF16).astype(F32)
    rest = v - hi
    mi = rest.astype(BF16).astype(F32)
    return hi, mi, rest - mi


def outer_sum(a, b):
    ah, am, al = split3(a)
    bh, bm, bl = split3(b)
    left = jnp.concatenate([ah, ah, am, am, ah, al], axis=0).astype(BF16)
    right = jnp.concatenate([bh, bm, bh, bm, bl, bh], axis=0).astype(BF16)
    return lax.dot_general(left, right, (((0,), (0,)), ((), ())), preferred_element_type=F32)


def tail_kernel(
    rows, red_ref, gram_ref, first_ref, second_ref, state_ref, reduced_ref, pod_ref, rhs_ref, final_ref, sem
):
    keep = pltpu.make_async_copy(state_ref, final_ref, sem)
    keep.start()
    l = lax.axis_index("learn")
    red = red_ref[...]
    row = lax.broadcasted_iota(jnp.int32, (8, 128), 0)
    lane = lax.broadcasted_iota(jnp.int32, (8, 128), 1)
    reduced_ref[...] = red[:, :MODES]
    pod_ref[...] = gram_ref[...] + outer_sum(red, red)[:MODES, :MODES]
    widened = jnp.where(lane == 0, 1.0, pltpu.roll(red, 1, 1))
    changes = jnp.where(row < STEPS - 1, pltpu.roll(red, 7, 0) - red, 0.0)
    feats = []
    for j in range(first_ref.shape[1]):
        one = jnp.broadcast_to(first_ref[l, pl.ds(j, 1), :], (8, 128))
        two = jnp.broadcast_to(second_ref[l, pl.ds(j, 1), :], (8, 128))
        feats.append(
            jnp.take_along_axis(widened, one, axis=1, mode="promise_in_bounds")
            * jnp.take_along_axis(widened, two, axis=1, mode="promise_in_bounds")
        )
    feats = jnp.concatenate(feats, axis=1)
    rhs_ref[...] = outer_sum(changes, feats)[:MODES, :rows]
    keep.wait()


def pair_tables(modes, blocks):
    upper_pairs = np.triu_indices(modes)
    first = np.concatenate([np.zeros(modes), upper_pairs[0] + 1]).astype(np.int32)
    second = np.concatenate([np.arange(modes) + 1, upper_pairs[1] + 1]).astype(np.int32)
    rows = first.shape[0] // blocks
    lines = -(-rows // 128)

    def lay(t):
        t = t.reshape(blocks, rows)
        t = np.pad(t, ((0, 0), (0, lines * 128 - rows)))
        return t.reshape(blocks, lines, 128)

    return rows, lay(first), lay(second)


def solution(mesh):
    sims, learns = mesh.shape["sim"], mesh.shape["learn"]
    dims = ((2, 4, 4), (2, 2)) if (sims, learns) == (32, 4) else ((1, 1, sims), (1, learns))
    (yh_n, z_n, x_n), (yl_n, core_n) = dims
    na, nb = x_n * core_n, yh_n * z_n * yl_n
    rows, first, second = pair_tables(MODES, learns)
    vmem = pl.BlockSpec(memory_space=pltpu.VMEM)
    hbm = pl.BlockSpec(memory_space=pl.ANY)
    n_pieces = len(PIECES)

    def body(fields, diffusivity, stoich, basis, gram_old):
        flat = basis.reshape(MODES, NF * CX * CY, 128)
        final, red = pl.pallas_call(
            functools.partial(steps_kernel, dims),
            out_shape=(
                jax.ShapeDtypeStruct((NF * CX, CY, 128), F32),
                jax.ShapeDtypeStruct((8, 128), F32),
            ),
            in_specs=[hbm] * 4,
            out_specs=(hbm, vmem),
            scratch_shapes=[
                pltpu.VMEM((2 * XB, YB * 8, 128), F32),
                pltpu.VMEM((XB, YB * 8, 128), F32),
                pltpu.VMEM((2 * XB, YB * 8, 128), F32),
                pltpu.VMEM((W * XB, -(-YB // 8) * 8, 128), F32),
                pltpu.VMEM((16, 128, 256), BF16),
                pltpu.VMEM((MODES, NF * CX * CY, 128), BF16),
                pltpu.VMEM((MODES * 16, 128), F32),
                pltpu.SMEM((NF,), F32),
                pltpu.SMEM((NF,), F32),
                pltpu.VMEM((NF * CX, CY, 128), F32),
                pltpu.SemaphoreType.DMA((3,)),
                pltpu.VMEM((2, 8, 128), F32),
                pltpu.VMEM((max(na - 1, 1), 8, 128), F32),
                pltpu.VMEM((max(nb - 1, 1), 8, 128), F32),
                pltpu.SemaphoreType.DMA,
                pltpu.SemaphoreType.DMA((2, n_pieces)),
                pltpu.SemaphoreType.DMA((2, n_pieces)),
                pltpu.SemaphoreType.DMA((max(na - 1, 1),)),
                pltpu.SemaphoreType.DMA((max(na - 1, 1),)),
                pltpu.SemaphoreType.DMA((max(nb - 1, 1),)),
                pltpu.SemaphoreType.DMA((max(nb - 1, 1),)),
            ],
            compiler_params=pltpu.CompilerParams(
                collective_id=0, has_side_effects=True, vmem_limit_bytes=60 * 1024 * 1024
            ),
            name="steps",
        )(diffusivity, stoich, fields.reshape(NF * CX, CY, 128), flat)
        reduced, pod, rhs, final = pl.pallas_call(
            functools.partial(tail_kernel, rows),
            out_shape=(
                jax.ShapeDtypeStruct((STEPS, MODES), F32),
                jax.ShapeDtypeStruct((MODES, MODES), F32),
                jax.ShapeDtypeStruct((MODES, rows), F32),
                jax.ShapeDtypeStruct((NF * CX, CY, 128), F32),
            ),
            in_specs=[vmem] * 5,
            out_specs=(vmem,) * 3 + (hbm,),
            scratch_shapes=[pltpu.SemaphoreType.DMA],
            compiler_params=pltpu.CompilerParams(vmem_limit_bytes=60 * 1024 * 1024),
            name="tail",
        )(red, gram_old, jnp.asarray(first), jnp.asarray(second), final)
        return final.reshape(NF, CX, CY, 128), reduced.T, pod, rhs.T

    in_specs = (
        P(None, "sim", "learn", None),
        P(),
        P(),
        P(None, None, "sim", "learn", None),
        P(),
    )
    out_specs = (P(None, "sim", "learn", None), P(), P(), P("learn", None))
    return jax.shard_map(body, mesh=mesh, in_specs=in_specs, out_specs=out_specs, check_vma=False)
```

```python
import functools

import jax
import jax.numpy as jnp
import numpy as np
from jax import lax
from jax.experimental import pallas as pl
from jax.experimental.pallas import tpu as pltpu
from jax.sharding import PartitionSpec as P

MESH = pl.DeviceIdType.MESH
STEPS = 8
PER = 4
W = 2 * PER
NF = 8
CX = 8
CY = 8
XB = CX + 2 * W
YB = CY + 2 * W
MODES = 96
F32 = jnp.float32
BF16 = jnp.bfloat16

time_step = 0.1
drift_x = 1.2
drift_y = 1.0
drift_z = 0.3
arrhenius = 2.0
activation = 1.0

DIRS = [(dx, dy) for dx in (-1, 0, 1) for dy in (-1, 0, 1) if (dx, dy) != (0, 0)]

GROUPS = ((1, 2), (3, 4), (5, 6), (7, 8))
NEAR = 2


def pieces():
    out, names = [], {}

    def add(name, *piece):
        names[name] = len(out)
        out.append(piece)

    def along_y(dy, n):
        return (W, W + CY) if dy < 0 else (W + CY - n, W - n)

    for g, (a, b) in enumerate(GROUPS):
        n = b - a + 1
        for dx in (-1, 1):
            sx, tx = (W + a - 1, W + CX + a - 1) if dx < 0 else (W + CX - b, W - b)
            add(("x", g, dx), dx, 0, 0, sx, W, tx, W, n, CY)
        if g == 0:
            for dy in (-1, 1):
                sy, ty = along_y(dy, CY)
                add(("y", dy), 0, dy, 0, W, sy, W, ty, CX, CY)
        rows = min(n, W - a)
        for dx in (-1, 1):
            sx, tx = (W + a - 1, W + CX + a - 1) if dx < 0 else (W + CX - a - rows + 1, W - a - rows + 1)
            for dy in (-1, 1):
                sy, ty = along_y(dy, W - a)
                add(("d", g, dx, dy), dx, dy, 0, sx, sy, tx, ty, rows, W - a)
    direct = len(out)
    for g, (a, b) in enumerate(GROUPS[:NEAR]):
        for side in (-1, 1):
            x = W - b if side < 0 else W + CX + a - 1
            for dy in (-1, 1):
                sy, ty = along_y(dy, W - a)
                add(("f", g, side, dy), 0, dy, side, x, sy, x, ty, b - a + 1, W - a)
    return out, names, direct


PIECES, NAMES, DIRECT = pieces()
FAR = [NAMES["d", g, dx, dy] for g in range(NEAR) for dx in (-1, 1) for dy in (-1, 1)]


def steps_kernel(
    dims,
    diff_hbm,
    stoich_hbm,
    fields_hbm,
    basis_ref,
    final_ref,
    red_ref,
    state,
    mid,
    later,
    rate,
    snaps,
    basis,
    acc,
    diff_ref,
    stoich_ref,
    fields_ref,
    in_sem,
    part,
    slots_a,
    slots_b,
    basis_sem,
    send_sem,
    recv_sem,
    send_a,
    recv_a,
    send_b,
    recv_b,
):
    (yh_n, z_n, x_n), (yl_n, core_n) = dims
    sims, learns = yh_n * z_n * x_n, yl_n * core_n
    s = lax.axis_index("sim")
    l = lax.axis_index("learn")

    fetch = pltpu.make_async_copy(basis_ref, basis, basis_sem)
    x_me = s % x_n
    z_me = (s // x_n) % z_n
    yh_me = s // (x_n * z_n)
    core_me = l % core_n
    yl_me = l // core_n

    peers_a = []
    na = x_n * core_n
    rank_a = x_me * core_n + core_me
    for k in range(1, na):
        r = (rank_a + k) % na
        peers_a.append(((s - x_me) + r // core_n, (l - core_me) + r % core_n))
    peers_b = []
    nb = yh_n * z_n * yl_n
    rank_b = (yh_me * z_n + z_me) * yl_n + yl_me
    for k in range(1, nb):
        r = (rank_b + k) % nb
        yz = r // yl_n
        peers_b.append((yz * x_n + x_me, (r % yl_n) * core_n + core_me))

    def there(dx, dy):
        ok = None
        for d, me, n in ((dx, s, sims), (dy, l, learns)):
            if d == 0:
                continue
            c = me > 0 if d < 0 else me < n - 1
            ok = c if ok is None else ok & c
        return ok

    def on_chip(dy, arriving):
        return core_me == (0 if (dy > 0) != arriving else 1)

    barrier = pltpu.get_barrier_semaphore()
    count = jnp.int32(len(peers_a) + len(peers_b))
    for dx, dy in DIRS:
        ok = there(dx, dy)
        count = count + ok.astype(jnp.int32)

        @pl.when(ok)
        def _(dx=dx, dy=dy):
            pl.semaphore_signal(
                barrier, inc=1, device_id={"sim": s + dx, "learn": l + dy}, device_id_type=MESH
            )

    for ps, pl_ in peers_a + peers_b:
        pl.semaphore_signal(barrier, inc=1, device_id={"sim": ps, "learn": pl_}, device_id_type=MESH)

    loads = [
        pltpu.make_async_copy(a, b, in_sem.at[i])
        for i, (a, b) in enumerate(
            ((fields_hbm, fields_ref), (diff_hbm, diff_ref), (stoich_hbm, stoich_ref))
        )
    ]
    for c in loads:
        c.start()
    fetch.start()

    for par in range(2):
        for edge, x in ((s == 0, par * XB), (s == lax.axis_size("sim") - 1, par * XB + W + CX)):

            @pl.when(edge)
            def _(x=x):
                state[pl.ds(x, W)] = jnp.zeros((W, YB * 8, 128), F32)

        for edge, y in ((l == 0, 0), (l == lax.axis_size("learn") - 1, W + CY)):

            @pl.when(edge)
            def _(par=par, y=y):
                state[pl.ds(par * XB, XB), pl.ds(y * 8, W * 8), :] = jnp.zeros((XB, W * 8, 128), F32)

    for c in loads:
        c.wait()

    for f in range(NF):
        for x in range(CX):
            state[W + x, pl.ds(W * 8 + f, 8, stride=8), :] = fields_ref[f * CX + x]

    row = lax.broadcasted_iota(jnp.int32, (8, 128), 0)
    lane = lax.broadcasted_iota(jnp.int32, (8, 128), 1)
    diff = jnp.zeros((8, 128), F32)
    sto = jnp.zeros((8, 128), F32)
    for f in range(NF):
        diff = jnp.where(row == f, diff_ref[f], diff)
        sto = jnp.where(row == f, stoich_ref[f], sto)

    def coefs(scale, keep):
        upper = jnp.where(lane < 127, scale * (diff - 0.5 * drift_z), 0.0)
        lower = jnp.where(lane > 0, scale * (diff + 0.5 * drift_z), 0.0)
        return (
            keep - (6.0 * scale) * diff,
            scale * (diff - 0.5 * drift_x),
            scale * (diff + 0.5 * drift_x),
            scale * (diff - 0.5 * drift_y),
            scale * (diff + 0.5 * drift_y),
            upper,
            lower,
            (scale * arrhenius) * sto,
        )

    coefs_1 = coefs(time_step, 1.0)
    coefs_2 = coefs(0.5 * time_step, 0.5)

    x_low = jnp.where(s > 0, 1.0, 0.0).astype(F32)
    x_high = jnp.where(s < sims - 1, 1.0, 0.0).astype(F32)
    y_low = jnp.where(l > 0, 1.0, 0.0).astype(F32)
    y_high = jnp.where(l < learns - 1, 1.0, 0.0).astype(F32)

    def beyond(x):
        return max(W - x, x - (W + CX - 1))

    def reach(s_, x):
        e = W - s_ - max(beyond(x), 0)
        return W - e, W + CY + e

    def rates(s_, src, base, x):
        y0, y1 = reach(s_, x)
        for y in sorted({min(y, y1 - 8) for y in range(y0, y1, 8)}):
            u0 = src[base + x, pl.ds(y * 8, 8, stride=8), :]
            u1 = src[base + x, pl.ds(y * 8 + 1, 8, stride=8), :]
            u7 = src[base + x, pl.ds(y * 8 + 7, 8, stride=8), :]
            rate[(s_ - 1) * XB + x, pl.ds(y, 8), :] = (
                jnp.tanh(u0) * jnp.tanh(u1) * jnp.exp(-activation / (1.0 + u7 * u7))
            )

    def cells(ref, x, y, n):
        return ref[x, pl.ds(y * 8, n * 8), :].reshape(n, 8, 128)

    def line(s_, src, base, dst, dbase, x, cs, old=None, obase=0):
        c_c, c_e, c_w, c_n, c_s, c_u, c_l, c_r = (c[None] for c in cs)
        y0, y1 = reach(s_, x)
        ends = sorted({y0, y1} | {y for y in (W, W + CY) if y0 < y < y1})
        for y, end in zip(ends[:-1], ends[1:]):
            n = end - y
            c = cells(src, base + x, y, n)
            q = jnp.stack(
                [
                    jnp.broadcast_to(rate[(s_ - 1) * XB + x, pl.ds(y + j, 1), :], (8, 128))
                    for j in range(n)
                ]
            )
            v = c_c * c + c_e * cells(src, base + x + 1, y, n)
            v = v + (c_w * cells(src, base + x - 1, y, n) + c_n * cells(src, base + x, y + 1, n))
            v = v + (c_s * cells(src, base + x, y - 1, n) + c_r * q)
            v = v + (c_u * pltpu.roll(c, 127, 2) + c_l * pltpu.roll(c, 1, 2))
            if old is not None:
                v = v + 0.5 * cells(old, obase + x, y, n)
            masks = []
            if x < W:
                masks.append(x_low)
            if x >= W + CX:
                masks.append(x_high)
            if y < W:
                masks.append(y_low)
            if y >= W + CY:
                masks.append(y_high)
            if masks:
                v = v * functools.reduce(lambda a, b: a * b, masks)
            dst[dbase + x, pl.ds(y * 8, n * 8), :] = v.reshape(n * 8, 128)

    def snapshot(src, base, t):
        for fp in range(NF // 2):
            for xp in range(CX // 2):
                halves = []
                for f in (2 * fp, 2 * fp + 1):
                    a = src[base + W + 2 * xp, pl.ds(W * 8 + f, 8, stride=8), :]
                    b = src[base + W + 2 * xp + 1, pl.ds(W * 8 + f, 8, stride=8), :]
                    halves.append(jnp.concatenate([a, b], axis=0))
                tile = jnp.concatenate(halves, axis=1).astype(BF16)
                snaps[fp * 4 + xp, pl.ds(pl.multiple_of(t * 16, 16), 16), :] = tile

    def copy(par, k):
        dx, dy, _, sx, sy, tx, ty, nx, ny = PIECES[k]
        return pltpu.make_async_remote_copy(
            src_ref=state.at[pl.ds(par * XB + sx, nx), pl.ds(sy * 8, ny * 8), :],
            dst_ref=state.at[pl.ds(par * XB + tx, nx), pl.ds(ty * 8, ny * 8), :],
            send_sem=send_sem.at[par, k],
            recv_sem=recv_sem.at[par, k],
            device_id={"sim": s + dx, "learn": l + dy},
            device_id_type=MESH,
        )

    pl.semaphore_wait(barrier, count)

    def each(par, chosen, act, arriving):
        for k in chosen:
            dx, dy, side = PIECES[k][:3]
            ok = there(-dx, -dy) if arriving else there(dx, dy)
            if side:
                ok = ok & there(side, 0) & on_chip(dy, arriving)
            if k in FAR:
                ok = ok & ~on_chip(dy, arriving)

            @pl.when(ok)
            def _(k=k):
                act(copy(par, k))

    def window(e, _):
        par = lax.rem(e, 2)
        base = par * XB
        nxt = (1 - par) * XB

        def send(chosen):
            each(par, chosen, lambda c: c.start(), False)

        def arrive(*names):
            each(par, [NAMES[n] for n in names], lambda c: c.wait_recv(), True)

        def held(s_):
            if s_ % 2:
                return mid, 0
            if s_ in (0, W):
                return state, (base if s_ == 0 else nxt)
            return later, (s_ // 2 % 2) * XB

        def level(i):
            todo = []
            for s_ in range(1, W + 1):
                for x in range(W - (W - s_), W + CX + (W - s_)):
                    need = max(s_ + beyond(x), 0)
                    if need == i:
                        todo.append((s_, x))
            if i > 0:
                for s_, x in todo:
                    rates(s_, *held(s_ - 1), x)
            done = 0
            for s_, x in todo:
                if i == 0 and s_ != done:
                    for t_, z in todo:
                        if t_ == s_:
                            rates(s_, *held(s_ - 1), z)
                    done = s_
                if s_ % 2:
                    line(s_, *held(s_ - 1), *held(s_), x, coefs_1)
                else:
                    line(s_, *held(s_ - 1), *held(s_), x, coefs_2, *held(s_ - 2))

        pairs = [(a, b) for a in (-1, 1) for b in (-1, 1)]
        arrive(("y", -1), ("y", 1))
        level(0)
        for g in range(NEAR):
            for dx in (-1, 1):
                arrive(("x", g, dx))
                send([NAMES["f", g, -dx, dy] for dy in (-1, 1)])
        for g, (a, b) in enumerate(GROUPS):
            if g < NEAR:
                arrive(*[("f", g, side, dy) for side, dy in pairs])
                arrive(*[("d", g, dx, dy) for dx, dy in pairs])
            else:
                arrive(("x", g, -1), ("x", g, 1), *[("d", g, dx, dy) for dx, dy in pairs])
            for i in range(a, b + 1):
                level(i)
                if i == W:

                    @pl.when(e < STEPS // PER - 1)
                    def _():
                        each(1 - par, range(DIRECT), lambda c: c.start(), False)

                if i % 2 == 0:
                    snapshot(*held(i), e * PER + i // 2 - 1)
        each(par, range(len(PIECES)), lambda c: c.wait_send(), False)
        return 0

    each(0, range(DIRECT), lambda c: c.start(), False)
    lax.fori_loop(0, STEPS // PER, window, 0)

    last = (STEPS // PER % 2) * XB
    for f in range(NF):
        for x in range(CX):
            fields_ref[f * CX + x] = state[last + W + x, pl.ds(W * 8 + f, 8, stride=8), :]
    keep = pltpu.make_async_copy(fields_ref, final_ref, in_sem.at[0])
    keep.start()

    fetch.wait()
    left, right = [], []
    for fp in range(NF // 2):
        for xp in range(CX // 2):
            for f in (2 * fp, 2 * fp + 1):
                rows = basis[:, pl.ds(f * CX * CY + xp * 16, 16), :]
                left.append(rows.reshape(MODES * 16, 128))
            right.append(snaps[fp * 4 + xp])
    acc[...] = lax.dot_general(
        jnp.concatenate(left, axis=1),
        jnp.concatenate(right, axis=1),
        (((1,), (1,)), ((), ())),
        preferred_element_type=F32,
    )

    r16 = lax.broadcasted_iota(jnp.int32, (16, 128), 0)
    c16 = lax.broadcasted_iota(jnp.int32, (16, 128), 1)
    diagonal = (c16 % 16 == r16).astype(F32)
    kept = jnp.sum(acc[...].reshape(MODES, 16, 128) * diagonal[None], axis=1)
    kept = jnp.concatenate([kept, jnp.zeros((128 - MODES, 128), F32)], axis=0)
    groups = (lane // 16 == row).astype(F32)
    mine = lax.dot_general(
        jnp.concatenate([groups] * 3, axis=1).astype(BF16),
        jnp.concatenate(split3(kept), axis=1).astype(BF16),
        (((1,), (1,)), ((), ())),
        preferred_element_type=F32,
    )

    def share(slots, peers, rank, n, phase, send, recv):
        copies = []
        for k, (ps, pl_) in enumerate(peers):
            c = pltpu.make_async_remote_copy(
                src_ref=part.at[phase],
                dst_ref=slots.at[k],
                send_sem=send.at[k],
                recv_sem=recv.at[k],
                device_id={"sim": ps, "learn": pl_},
                device_id_type=MESH,
            )
            c.start()
            copies.append(c)
        for c in copies:
            c.wait()

    def total(slots, rank, n, phase):
        out = jnp.zeros((8, 128), F32)
        for r in range(n):
            k = lax.rem(rank - r + n - 1 + n, n)
            mine_now = part[phase]
            other = slots[jnp.minimum(k, n - 2)]
            out = out + jnp.where(rank == r, mine_now, other)
        return out

    part[0] = mine
    share(slots_a, peers_a, rank_a, na, 0, send_a, recv_a)
    part[1] = total(slots_a, rank_a, na, 0)
    share(slots_b, peers_b, rank_b, nb, 1, send_b, recv_b)
    red_ref[...] = total(slots_b, rank_b, nb, 1)
    keep.wait()


def split3(v):
    hi = v.astype(BF16).astype(F32)
    rest = v - hi
    mi = rest.astype(BF16).astype(F32)
    return hi, mi, rest - mi


def outer_sum(a, b):
    ah, am, al = split3(a)
    bh, bm, bl = split3(b)
    left = jnp.concatenate([ah, ah, am, am, ah, al], axis=0).astype(BF16)
    right = jnp.concatenate([bh, bm, bh, bm, bl, bh], axis=0).astype(BF16)
    return lax.dot_general(left, right, (((0,), (0,)), ((), ())), preferred_element_type=F32)


def tail_kernel(
    rows, red_ref, gram_ref, first_ref, second_ref, state_ref, reduced_ref, pod_ref, rhs_ref, final_ref, sem
):
    keep = pltpu.make_async_copy(state_ref, final_ref, sem)
    keep.start()
    l = lax.axis_index("learn")
    red = red_ref[...]
    row = lax.broadcasted_iota(jnp.int32, (8, 128), 0)
    lane = lax.broadcasted_iota(jnp.int32, (8, 128), 1)
    reduced_ref[...] = red[:, :MODES]
    pod_ref[...] = gram_ref[...] + outer_sum(red, red)[:MODES, :MODES]
    widened = jnp.where(lane == 0, 1.0, pltpu.roll(red, 1, 1))
    changes = jnp.where(row < STEPS - 1, pltpu.roll(red, 7, 0) - red, 0.0)
    feats = []
    for j in range(first_ref.shape[1]):
        one = jnp.broadcast_to(first_ref[l, pl.ds(j, 1), :], (8, 128))
        two = jnp.broadcast_to(second_ref[l, pl.ds(j, 1), :], (8, 128))
        feats.append(
            jnp.take_along_axis(widened, one, axis=1, mode="promise_in_bounds")
            * jnp.take_along_axis(widened, two, axis=1, mode="promise_in_bounds")
        )
    feats = jnp.concatenate(feats, axis=1)
    rhs_ref[...] = outer_sum(changes, feats)[:MODES, :rows]
    keep.wait()


def pair_tables(modes, blocks):
    upper_pairs = np.triu_indices(modes)
    first = np.concatenate([np.zeros(modes), upper_pairs[0] + 1]).astype(np.int32)
    second = np.concatenate([np.arange(modes) + 1, upper_pairs[1] + 1]).astype(np.int32)
    rows = first.shape[0] // blocks
    lines = -(-rows // 128)

    def lay(t):
        t = t.reshape(blocks, rows)
        t = np.pad(t, ((0, 0), (0, lines * 128 - rows)))
        return t.reshape(blocks, lines, 128)

    return rows, lay(first), lay(second)


def solution(mesh):
    sims, learns = mesh.shape["sim"], mesh.shape["learn"]
    dims = ((2, 4, 4), (2, 2)) if (sims, learns) == (32, 4) else ((1, 1, sims), (1, learns))
    (yh_n, z_n, x_n), (yl_n, core_n) = dims
    na, nb = x_n * core_n, yh_n * z_n * yl_n
    rows, first, second = pair_tables(MODES, learns)
    vmem = pl.BlockSpec(memory_space=pltpu.VMEM)
    hbm = pl.BlockSpec(memory_space=pl.ANY)
    n_pieces = len(PIECES)

    def body(fields, diffusivity, stoich, basis, gram_old):
        flat = basis.reshape(MODES, NF * CX * CY, 128)
        final, red = pl.pallas_call(
            functools.partial(steps_kernel, dims),
            out_shape=(
                jax.ShapeDtypeStruct((NF * CX, CY, 128), F32),
                jax.ShapeDtypeStruct((8, 128), F32),
            ),
            in_specs=[hbm] * 4,
            out_specs=(hbm, vmem),
            scratch_shapes=[
                pltpu.VMEM((2 * XB, YB * 8, 128), F32),
                pltpu.VMEM((XB, YB * 8, 128), F32),
                pltpu.VMEM((2 * XB, YB * 8, 128), F32),
                pltpu.VMEM((W * XB, -(-YB // 8) * 8, 128), F32),
                pltpu.VMEM((16, 128, 256), BF16),
                pltpu.VMEM((MODES, NF * CX * CY, 128), BF16),
                pltpu.VMEM((MODES * 16, 128), F32),
                pltpu.SMEM((NF,), F32),
                pltpu.SMEM((NF,), F32),
                pltpu.VMEM((NF * CX, CY, 128), F32),
                pltpu.SemaphoreType.DMA((3,)),
                pltpu.VMEM((2, 8, 128), F32),
                pltpu.VMEM((max(na - 1, 1), 8, 128), F32),
                pltpu.VMEM((max(nb - 1, 1), 8, 128), F32),
                pltpu.SemaphoreType.DMA,
                pltpu.SemaphoreType.DMA((2, n_pieces)),
                pltpu.SemaphoreType.DMA((2, n_pieces)),
                pltpu.SemaphoreType.DMA((max(na - 1, 1),)),
                pltpu.SemaphoreType.DMA((max(na - 1, 1),)),
                pltpu.SemaphoreType.DMA((max(nb - 1, 1),)),
                pltpu.SemaphoreType.DMA((max(nb - 1, 1),)),
            ],
            compiler_params=pltpu.CompilerParams(
                collective_id=0, has_side_effects=True, vmem_limit_bytes=60 * 1024 * 1024
            ),
            name="steps",
        )(diffusivity, stoich, fields.reshape(NF * CX, CY, 128), flat)
        reduced, pod, rhs, final = pl.pallas_call(
            functools.partial(tail_kernel, rows),
            out_shape=(
                jax.ShapeDtypeStruct((STEPS, MODES), F32),
                jax.ShapeDtypeStruct((MODES, MODES), F32),
                jax.ShapeDtypeStruct((MODES, rows), F32),
                jax.ShapeDtypeStruct((NF * CX, CY, 128), F32),
            ),
            in_specs=[vmem] * 5,
            out_specs=(vmem,) * 3 + (hbm,),
            scratch_shapes=[pltpu.SemaphoreType.DMA],
            compiler_params=pltpu.CompilerParams(vmem_limit_bytes=60 * 1024 * 1024),
            name="tail",
        )(red, gram_old, jnp.asarray(first), jnp.asarray(second), final)
        return final.reshape(NF, CX, CY, 128), reduced.T, pod, rhs.T

    in_specs = (
        P(None, "sim", "learn", None),
        P(),
        P(),
        P(None, None, "sim", "learn", None),
        P(),
    )
    out_specs = (P(None, "sim", "learn", None), P(), P(), P("learn", None))
    return jax.shard_map(body, mesh=mesh, in_specs=in_specs, out_specs=out_specs, check_vma=False)
```

```python
import functools

import jax
import jax.numpy as jnp
import numpy as np
from jax import lax
from jax.experimental import pallas as pl
from jax.experimental.pallas import tpu as pltpu
from jax.sharding import PartitionSpec as P

MESH = pl.DeviceIdType.MESH
STEPS = 8
PER = 4
W = 2 * PER
NF = 8
CX = 8
CY = 8
XB = CX + 2 * W
YB = CY + 2 * W
MODES = 96
F32 = jnp.float32
BF16 = jnp.bfloat16

time_step = 0.1
drift_x = 1.2
drift_y = 1.0
drift_z = 0.3
arrhenius = 2.0
activation = 1.0

DIRS = [(dx, dy) for dx in (-1, 0, 1) for dy in (-1, 0, 1) if (dx, dy) != (0, 0)]

GROUPS = ((1, 2), (3, 4), (5, 6), (7, 8))
NEAR = 2


def pieces():
    out, names = [], {}

    def add(name, *piece):
        names[name] = len(out)
        out.append(piece)

    def along_y(dy, n):
        return (W, W + CY) if dy < 0 else (W + CY - n, W - n)

    for g, (a, b) in enumerate(GROUPS):
        n = b - a + 1
        for dx in (-1, 1):
            sx, tx = (W + a - 1, W + CX + a - 1) if dx < 0 else (W + CX - b, W - b)
            add(("x", g, dx), dx, 0, 0, sx, W, tx, W, n, CY)
        if g == 0:
            for dy in (-1, 1):
                sy, ty = along_y(dy, CY)
                add(("y", dy), 0, dy, 0, W, sy, W, ty, CX, CY)
        rows = min(n, W - a)
        for dx in (-1, 1):
            sx, tx = (W + a - 1, W + CX + a - 1) if dx < 0 else (W + CX - a - rows + 1, W - a - rows + 1)
            for dy in (-1, 1):
                sy, ty = along_y(dy, W - a)
                add(("d", g, dx, dy), dx, dy, 0, sx, sy, tx, ty, rows, W - a)
    direct = len(out)
    for g, (a, b) in enumerate(GROUPS[:NEAR]):
        for side in (-1, 1):
            x = W - b if side < 0 else W + CX + a - 1
            for dy in (-1, 1):
                sy, ty = along_y(dy, W - a)
                add(("f", g, side, dy), 0, dy, side, x, sy, x, ty, b - a + 1, W - a)
    return out, names, direct


PIECES, NAMES, DIRECT = pieces()
FAR = [NAMES["d", g, dx, dy] for g in range(NEAR) for dx in (-1, 1) for dy in (-1, 1)]


def steps_kernel(
    dims,
    diff_hbm,
    stoich_hbm,
    fields_hbm,
    basis_ref,
    final_ref,
    red_ref,
    state,
    mid,
    later,
    rate,
    snaps,
    basis,
    acc,
    diff_ref,
    stoich_ref,
    fields_ref,
    in_sem,
    part,
    slots_a,
    slots_b,
    basis_sem,
    send_sem,
    recv_sem,
    send_a,
    recv_a,
    send_b,
    recv_b,
):
    (yh_n, z_n, x_n), (yl_n, core_n) = dims
    sims, learns = yh_n * z_n * x_n, yl_n * core_n
    s = lax.axis_index("sim")
    l = lax.axis_index("learn")

    fetch = pltpu.make_async_copy(basis_ref, basis, basis_sem)
    x_me = s % x_n
    z_me = (s // x_n) % z_n
    yh_me = s // (x_n * z_n)
    core_me = l % core_n
    yl_me = l // core_n

    peers_a = []
    na = x_n * core_n
    rank_a = x_me * core_n + core_me
    for k in range(1, na):
        r = (rank_a + k) % na
        peers_a.append(((s - x_me) + r // core_n, (l - core_me) + r % core_n))
    peers_b = []
    nb = yh_n * z_n * yl_n
    rank_b = (yh_me * z_n + z_me) * yl_n + yl_me
    for k in range(1, nb):
        r = (rank_b + k) % nb
        yz = r // yl_n
        peers_b.append((yz * x_n + x_me, (r % yl_n) * core_n + core_me))

    def there(dx, dy):
        ok = None
        for d, me, n in ((dx, s, sims), (dy, l, learns)):
            if d == 0:
                continue
            c = me > 0 if d < 0 else me < n - 1
            ok = c if ok is None else ok & c
        return ok

    def on_chip(dy, arriving):
        return core_me == (0 if (dy > 0) != arriving else 1)

    barrier = pltpu.get_barrier_semaphore()
    count = jnp.int32(len(peers_a) + len(peers_b))
    for dx, dy in DIRS:
        ok = there(dx, dy)
        count = count + ok.astype(jnp.int32)

        @pl.when(ok)
        def _(dx=dx, dy=dy):
            pl.semaphore_signal(
                barrier, inc=1, device_id={"sim": s + dx, "learn": l + dy}, device_id_type=MESH
            )

    for ps, pl_ in peers_a + peers_b:
        pl.semaphore_signal(barrier, inc=1, device_id={"sim": ps, "learn": pl_}, device_id_type=MESH)

    loads = [
        pltpu.make_async_copy(a, b, in_sem.at[i])
        for i, (a, b) in enumerate(
            ((fields_hbm, fields_ref), (diff_hbm, diff_ref), (stoich_hbm, stoich_ref))
        )
    ]
    for c in loads:
        c.start()
    fetch.start()

    for par in range(2):
        for edge, x in ((s == 0, par * XB), (s == lax.axis_size("sim") - 1, par * XB + W + CX)):

            @pl.when(edge)
            def _(x=x):
                state[pl.ds(x, W)] = jnp.zeros((W, YB * 8, 128), F32)

        for edge, y in ((l == 0, 0), (l == lax.axis_size("learn") - 1, W + CY)):

            @pl.when(edge)
            def _(par=par, y=y):
                state[pl.ds(par * XB, XB), pl.ds(y * 8, W * 8), :] = jnp.zeros((XB, W * 8, 128), F32)

    for c in loads:
        c.wait()

    for f in range(NF):
        for x in range(CX):
            state[W + x, pl.ds(W * 8 + f, 8, stride=8), :] = fields_ref[f * CX + x]

    row = lax.broadcasted_iota(jnp.int32, (8, 128), 0)
    lane = lax.broadcasted_iota(jnp.int32, (8, 128), 1)
    diff = jnp.zeros((8, 128), F32)
    sto = jnp.zeros((8, 128), F32)
    for f in range(NF):
        diff = jnp.where(row == f, diff_ref[f], diff)
        sto = jnp.where(row == f, stoich_ref[f], sto)

    def coefs(scale, keep):
        upper = jnp.where(lane < 127, scale * (diff - 0.5 * drift_z), 0.0)
        lower = jnp.where(lane > 0, scale * (diff + 0.5 * drift_z), 0.0)
        return (
            keep - (6.0 * scale) * diff,
            scale * (diff - 0.5 * drift_x),
            scale * (diff + 0.5 * drift_x),
            scale * (diff - 0.5 * drift_y),
            scale * (diff + 0.5 * drift_y),
            upper,
            lower,
            (scale * arrhenius) * sto,
        )

    coefs_1 = coefs(time_step, 1.0)
    coefs_2 = coefs(0.5 * time_step, 0.5)

    x_low = jnp.where(s > 0, 1.0, 0.0).astype(F32)
    x_high = jnp.where(s < sims - 1, 1.0, 0.0).astype(F32)
    y_low = jnp.where(l > 0, 1.0, 0.0).astype(F32)
    y_high = jnp.where(l < learns - 1, 1.0, 0.0).astype(F32)

    def beyond(x):
        return max(W - x, x - (W + CX - 1))

    def reach(s_, x):
        e = W - s_ - max(beyond(x), 0)
        return W - e, W + CY + e

    def rates(s_, src, base, x):
        y0, y1 = reach(s_, x)
        for y in sorted({min(y, y1 - 8) for y in range(y0, y1, 8)}):
            u0 = src[base + x, pl.ds(y * 8, 8, stride=8), :]
            u1 = src[base + x, pl.ds(y * 8 + 1, 8, stride=8), :]
            u7 = src[base + x, pl.ds(y * 8 + 7, 8, stride=8), :]
            rate[(s_ - 1) * XB + x, pl.ds(y, 8), :] = (
                jnp.tanh(u0) * jnp.tanh(u1) * jnp.exp(-activation / (1.0 + u7 * u7))
            )

    def cells(ref, x, y, n):
        return ref[x, pl.ds(y * 8, n * 8), :].reshape(n, 8, 128)

    def line(s_, src, base, dst, dbase, x, cs, old=None, obase=0):
        c_c, c_e, c_w, c_n, c_s, c_u, c_l, c_r = (c[None] for c in cs)
        y0, y1 = reach(s_, x)
        ends = sorted({y0, y1} | {y for y in (W, W + CY) if y0 < y < y1})
        for y, end in zip(ends[:-1], ends[1:]):
            n = end - y
            c = cells(src, base + x, y, n)
            q = jnp.stack(
                [
                    jnp.broadcast_to(rate[(s_ - 1) * XB + x, pl.ds(y + j, 1), :], (8, 128))
                    for j in range(n)
                ]
            )
            v = c_c * c + c_e * cells(src, base + x + 1, y, n)
            v = v + (c_w * cells(src, base + x - 1, y, n) + c_n * cells(src, base + x, y + 1, n))
            v = v + (c_s * cells(src, base + x, y - 1, n) + c_r * q)
            v = v + (c_u * pltpu.roll(c, 127, 2) + c_l * pltpu.roll(c, 1, 2))
            if old is not None:
                v = v + 0.5 * cells(old, obase + x, y, n)
            masks = []
            if x < W:
                masks.append(x_low)
            if x >= W + CX:
                masks.append(x_high)
            if y < W:
                masks.append(y_low)
            if y >= W + CY:
                masks.append(y_high)
            if masks:
                v = v * functools.reduce(lambda a, b: a * b, masks)
            dst[dbase + x, pl.ds(y * 8, n * 8), :] = v.reshape(n * 8, 128)

    def snapshot(src, base, t):
        for fp in range(NF // 2):
            for xp in range(CX // 2):
                halves = []
                for f in (2 * fp, 2 * fp + 1):
                    a = src[base + W + 2 * xp, pl.ds(W * 8 + f, 8, stride=8), :]
                    b = src[base + W + 2 * xp + 1, pl.ds(W * 8 + f, 8, stride=8), :]
                    halves.append(jnp.concatenate([a, b], axis=0))
                tile = jnp.concatenate(halves, axis=1).astype(BF16)
                snaps[fp * 4 + xp, pl.ds(pl.multiple_of(t * 16, 16), 16), :] = tile

    def copy(par, k):
        dx, dy, _, sx, sy, tx, ty, nx, ny = PIECES[k]
        return pltpu.make_async_remote_copy(
            src_ref=state.at[pl.ds(par * XB + sx, nx), pl.ds(sy * 8, ny * 8), :],
            dst_ref=state.at[pl.ds(par * XB + tx, nx), pl.ds(ty * 8, ny * 8), :],
            send_sem=send_sem.at[par, k],
            recv_sem=recv_sem.at[par, k],
            device_id={"sim": s + dx, "learn": l + dy},
            device_id_type=MESH,
        )

    pl.semaphore_wait(barrier, count)

    def each(par, chosen, act, arriving):
        for k in chosen:
            dx, dy, side = PIECES[k][:3]
            ok = there(-dx, -dy) if arriving else there(dx, dy)
            if side:
                ok = ok & there(side, 0) & on_chip(dy, arriving)
            if k in FAR:
                ok = ok & ~on_chip(dy, arriving)

            @pl.when(ok)
            def _(k=k):
                act(copy(par, k))

    def window(e, _):
        par = lax.rem(e, 2)
        base = par * XB
        nxt = (1 - par) * XB

        def send(chosen):
            each(par, chosen, lambda c: c.start(), False)

        def arrive(*names):
            each(par, [NAMES[n] for n in names], lambda c: c.wait_recv(), True)

        def held(s_):
            if s_ % 2:
                return mid, 0
            if s_ in (0, W):
                return state, (base if s_ == 0 else nxt)
            return later, (s_ // 2 % 2) * XB

        def level(i):
            todo = []
            for s_ in range(1, W + 1):
                for x in range(W - (W - s_), W + CX + (W - s_)):
                    need = max(s_ + beyond(x), 0)
                    if need == i:
                        todo.append((s_, x))
            if i > 0:
                for s_, x in todo:
                    rates(s_, *held(s_ - 1), x)
            done = 0
            for s_, x in todo:
                if i == 0 and s_ != done:
                    for t_, z in todo:
                        if t_ == s_:
                            rates(s_, *held(s_ - 1), z)
                    done = s_
                if s_ % 2:
                    line(s_, *held(s_ - 1), *held(s_), x, coefs_1)
                else:
                    line(s_, *held(s_ - 1), *held(s_), x, coefs_2, *held(s_ - 2))

        pairs = [(a, b) for a in (-1, 1) for b in (-1, 1)]
        arrive(("y", -1), ("y", 1))
        level(0)
        for g in range(NEAR):
            for dx in (-1, 1):
                arrive(("x", g, dx))
                send([NAMES["f", g, -dx, dy] for dy in (-1, 1)])
        for g, (a, b) in enumerate(GROUPS):
            if g < NEAR:
                arrive(*[("f", g, side, dy) for side, dy in pairs])
                arrive(*[("d", g, dx, dy) for dx, dy in pairs])
            else:
                arrive(("x", g, -1), ("x", g, 1), *[("d", g, dx, dy) for dx, dy in pairs])
            for i in range(a, b + 1):
                level(i)
                if i == W:

                    @pl.when(e < STEPS // PER - 1)
                    def _():
                        each(1 - par, range(DIRECT), lambda c: c.start(), False)

                if i % 2 == 0:
                    snapshot(*held(i), e * PER + i // 2 - 1)
        each(par, range(len(PIECES)), lambda c: c.wait_send(), False)
        return 0

    each(0, range(DIRECT), lambda c: c.start(), False)
    lax.fori_loop(0, STEPS // PER, window, 0)

    last = (STEPS // PER % 2) * XB
    for f in range(NF):
        for x in range(CX):
            fields_ref[f * CX + x] = state[last + W + x, pl.ds(W * 8 + f, 8, stride=8), :]
    keep = pltpu.make_async_copy(fields_ref, final_ref, in_sem.at[0])
    keep.start()

    fetch.wait()
    left, right = [], []
    for fp in range(NF // 2):
        for xp in range(CX // 2):
            for f in (2 * fp, 2 * fp + 1):
                rows = basis[:, pl.ds(f * CX * CY + xp * 16, 16), :]
                left.append(rows.reshape(MODES * 16, 128))
            right.append(snaps[fp * 4 + xp])
    acc[...] = lax.dot_general(
        jnp.concatenate(left, axis=1),
        jnp.concatenate(right, axis=1),
        (((1,), (1,)), ((), ())),
        preferred_element_type=F32,
    )

    r16 = lax.broadcasted_iota(jnp.int32, (16, 128), 0)
    c16 = lax.broadcasted_iota(jnp.int32, (16, 128), 1)
    diagonal = (c16 % 16 == r16).astype(F32)
    kept = jnp.sum(acc[...].reshape(MODES, 16, 128) * diagonal[None], axis=1)
    kept = jnp.concatenate([kept, jnp.zeros((128 - MODES, 128), F32)], axis=0)
    groups = (lane // 16 == row).astype(F32)
    mine = lax.dot_general(
        jnp.concatenate([groups] * 3, axis=1).astype(BF16),
        jnp.concatenate(split3(kept), axis=1).astype(BF16),
        (((1,), (1,)), ((), ())),
        preferred_element_type=F32,
    )

    def share(slots, peers, rank, n, phase, send, recv):
        copies = []
        for k, (ps, pl_) in enumerate(peers):
            c = pltpu.make_async_remote_copy(
                src_ref=part.at[phase],
                dst_ref=slots.at[k],
                send_sem=send.at[k],
                recv_sem=recv.at[k],
                device_id={"sim": ps, "learn": pl_},
                device_id_type=MESH,
            )
            c.start()
            copies.append(c)
        for c in copies:
            c.wait()

    def total(slots, rank, n, phase):
        out = jnp.zeros((8, 128), F32)
        for r in range(n):
            k = lax.rem(rank - r + n - 1 + n, n)
            mine_now = part[phase]
            other = slots[jnp.minimum(k, n - 2)]
            out = out + jnp.where(rank == r, mine_now, other)
        return out

    part[0] = mine
    share(slots_a, peers_a, rank_a, na, 0, send_a, recv_a)
    part[1] = total(slots_a, rank_a, na, 0)
    share(slots_b, peers_b, rank_b, nb, 1, send_b, recv_b)
    red_ref[...] = total(slots_b, rank_b, nb, 1)
    keep.wait()


def split3(v):
    hi = v.astype(BF16).astype(F32)
    rest = v - hi
    mi = rest.astype(BF16).astype(F32)
    return hi, mi, rest - mi


def outer_sum(a, b):
    ah, am, al = split3(a)
    bh, bm, bl = split3(b)
    left = jnp.concatenate([ah, ah, am, am, ah, al], axis=0).astype(BF16)
    right = jnp.concatenate([bh, bm, bh, bm, bl, bh], axis=0).astype(BF16)
    return lax.dot_general(left, right, (((0,), (0,)), ((), ())), preferred_element_type=F32)


def tail_kernel(
    rows, red_ref, gram_ref, tables_ref, state_ref, reduced_ref, pod_ref, rhs_ref, final_ref, sem
):
    keep = pltpu.make_async_copy(state_ref, final_ref, sem)
    keep.start()
    l = lax.axis_index("learn")
    red = red_ref[...]
    row = lax.broadcasted_iota(jnp.int32, (8, 128), 0)
    lane = lax.broadcasted_iota(jnp.int32, (8, 128), 1)
    reduced_ref[...] = red[:, :MODES]
    pod_ref[...] = gram_ref[...] + outer_sum(red, red)[:MODES, :MODES]
    widened = jnp.where(lane == 0, 1.0, pltpu.roll(red, 1, 1))
    changes = jnp.where(row < STEPS - 1, pltpu.roll(red, 7, 0) - red, 0.0)
    feats = []
    for j in range(tables_ref.shape[2]):
        one = jnp.broadcast_to(tables_ref[0, l, pl.ds(j, 1), :], (8, 128))
        two = jnp.broadcast_to(tables_ref[1, l, pl.ds(j, 1), :], (8, 128))
        feats.append(
            jnp.take_along_axis(widened, one, axis=1, mode="promise_in_bounds")
            * jnp.take_along_axis(widened, two, axis=1, mode="promise_in_bounds")
        )
    feats = jnp.concatenate(feats, axis=1)
    rhs_ref[...] = outer_sum(changes, feats)[:MODES, :rows]
    keep.wait()


def pair_tables(modes, blocks):
    upper_pairs = np.triu_indices(modes)
    first = np.concatenate([np.zeros(modes), upper_pairs[0] + 1]).astype(np.int32)
    second = np.concatenate([np.arange(modes) + 1, upper_pairs[1] + 1]).astype(np.int32)
    rows = first.shape[0] // blocks
    lines = -(-rows // 128)

    def lay(t):
        t = t.reshape(blocks, rows)
        t = np.pad(t, ((0, 0), (0, lines * 128 - rows)))
        return t.reshape(blocks, lines, 128)

    return rows, lay(first), lay(second)


def solution(mesh):
    sims, learns = mesh.shape["sim"], mesh.shape["learn"]
    dims = ((2, 4, 4), (2, 2)) if (sims, learns) == (32, 4) else ((1, 1, sims), (1, learns))
    (yh_n, z_n, x_n), (yl_n, core_n) = dims
    na, nb = x_n * core_n, yh_n * z_n * yl_n
    rows, first, second = pair_tables(MODES, learns)
    vmem = pl.BlockSpec(memory_space=pltpu.VMEM)
    hbm = pl.BlockSpec(memory_space=pl.ANY)
    n_pieces = len(PIECES)

    def body(fields, diffusivity, stoich, basis, gram_old):
        flat = basis.reshape(MODES, NF * CX * CY, 128)
        final, red = pl.pallas_call(
            functools.partial(steps_kernel, dims),
            out_shape=(
                jax.ShapeDtypeStruct((NF * CX, CY, 128), F32),
                jax.ShapeDtypeStruct((8, 128), F32),
            ),
            in_specs=[hbm] * 4,
            out_specs=(hbm, vmem),
            scratch_shapes=[
                pltpu.VMEM((2 * XB, YB * 8, 128), F32),
                pltpu.VMEM((XB, YB * 8, 128), F32),
                pltpu.VMEM((2 * XB, YB * 8, 128), F32),
                pltpu.VMEM((W * XB, -(-YB // 8) * 8, 128), F32),
                pltpu.VMEM((16, 128, 256), BF16),
                pltpu.VMEM((MODES, NF * CX * CY, 128), BF16),
                pltpu.VMEM((MODES * 16, 128), F32),
                pltpu.SMEM((NF,), F32),
                pltpu.SMEM((NF,), F32),
                pltpu.VMEM((NF * CX, CY, 128), F32),
                pltpu.SemaphoreType.DMA((3,)),
                pltpu.VMEM((2, 8, 128), F32),
                pltpu.VMEM((max(na - 1, 1), 8, 128), F32),
                pltpu.VMEM((max(nb - 1, 1), 8, 128), F32),
                pltpu.SemaphoreType.DMA,
                pltpu.SemaphoreType.DMA((2, n_pieces)),
                pltpu.SemaphoreType.DMA((2, n_pieces)),
                pltpu.SemaphoreType.DMA((max(na - 1, 1),)),
                pltpu.SemaphoreType.DMA((max(na - 1, 1),)),
                pltpu.SemaphoreType.DMA((max(nb - 1, 1),)),
                pltpu.SemaphoreType.DMA((max(nb - 1, 1),)),
            ],
            compiler_params=pltpu.CompilerParams(
                collective_id=0, has_side_effects=True, vmem_limit_bytes=60 * 1024 * 1024
            ),
            name="steps",
        )(diffusivity, stoich, fields.reshape(NF * CX, CY, 128), flat)
        reduced, pod, rhs, final = pl.pallas_call(
            functools.partial(tail_kernel, rows),
            out_shape=(
                jax.ShapeDtypeStruct((STEPS, MODES), F32),
                jax.ShapeDtypeStruct((MODES, MODES), F32),
                jax.ShapeDtypeStruct((MODES, rows), F32),
                jax.ShapeDtypeStruct((NF * CX, CY, 128), F32),
            ),
            in_specs=[vmem] * 4,
            out_specs=(vmem,) * 3 + (hbm,),
            scratch_shapes=[pltpu.SemaphoreType.DMA],
            compiler_params=pltpu.CompilerParams(vmem_limit_bytes=60 * 1024 * 1024),
            name="tail",
        )(red, gram_old, jnp.asarray(np.stack([first, second])), final)
        return final.reshape(NF, CX, CY, 128), reduced.T, pod, rhs.T

    in_specs = (
        P(None, "sim", "learn", None),
        P(),
        P(),
        P(None, None, "sim", "learn", None),
        P(),
    )
    out_specs = (P(None, "sim", "learn", None), P(), P(), P("learn", None))
    return jax.shard_map(body, mesh=mesh, in_specs=in_specs, out_specs=out_specs, check_vma=False)
```
